32 devices in a mesh: outer: 8 (over y, x, core), inner: 4 (over z).
Axes of the slice: x: 2, y: 2, z: 4, core: 2. Of those that a mesh axis runs over, the one named last changes fastest.
Arguments:
- queries: bfloat16 [4096, 768], P(('outer', 'inner')), may hold values from -5.5 to 5.5
- keys: bfloat16 [4096, 128], P(('outer', 'inner')), may hold values from -5.5 to 5.5
- values: bfloat16 [4096, 128], P(('outer', 'inner')), may hold values from -6 to 6
- grad_out: bfloat16 [4096, 768], P(('outer', 'inner')), may hold values from -96 to 96
- span_slot: int32 [64], replicated, may hold values from 0 to 63, as said below
Outputs:
- grad_queries: bfloat16 [4096, 768], P(('outer', 'inner'))
- grad_keys: bfloat16 [4096, 128], P(('outer', 'inner'))
- grad_values: bfloat16 [4096, 128], P(('outer', 'inner'))
The draws below stay inside these ranges and needn't reach their ends.
Inputs may be any that keep to these rules, and one draw needn't show every extreme that they name: `span_slot`: slots 2 d and 2 d + 1 hold spans c and 63 - c for some c below 32; every span is held once.
All inputs are finite; a program needn't handle non-finite values.
Results may differ from the reference program's by a relative error of at most 0.0074.
Values may be sent and summed in bfloat16 or wider, within the bound.
A program may use at most 128 MiB of HBM per device.

```python
import math
import jax
import jax.numpy as jnp
from jax import lax

HD = 128
GROUP = 6
TOKENS = 4096
SPANS = 64


def draw_queries(key, part):
    key = jax.random.fold_in(key, 3)
    base = jnp.clip(jax.random.normal(key, (TOKENS, GROUP * HD), jnp.float32), -4.5, 4.5)
    return base.astype(jnp.bfloat16)


def draw_keys(key, part):
    key = jax.random.fold_in(key, 5)
    base = jnp.clip(jax.random.normal(key, (TOKENS, HD), jnp.float32), -4.5, 4.5)
    return base.astype(jnp.bfloat16)


def draw_span_slot(key, part):
    key = jax.random.fold_in(key, 7)
    half = SPANS // 2
    order = jax.random.permutation(key, half).astype(jnp.int32)
    paired = jnp.stack([order, SPANS - 1 - order], axis=1)
    return paired.reshape(-1).astype(jnp.int32)


def levels(rng, shape, pieces, smallest, largest):
    level, own = 1.0, jax.random.fold_in(rng, 6)
    for dim, shards_of in pieces:
        heights = jnp.exp(jax.random.uniform(jax.random.fold_in(own, dim), (shards_of,), jnp.float32, smallest / len(pieces), largest / len(pieces)))
        level = level * jnp.repeat(heights, shape[dim] // shards_of).reshape([-1 if axis == dim else 1 for axis in range(len(shape))])
    return level


def normal_values(stream_key, dims, spread, bound, pieces=(), kind=jnp.bfloat16):
    entries = jax.random.normal(stream_key, dims, jnp.float32) * spread
    if len(pieces) > 0:
        entries = levels(stream_key, dims, pieces, -0.22, 0.18) * entries
    return jnp.clip(entries, min=-bound, max=bound).astype(kind)


def setup_inputs(seed: int = 0) -> dict:
    arg_keys = jax.random.split(jax.random.key(seed), 6)
    queries = draw_queries(jax.random.fold_in(arg_keys[5], 71), 0)
    keys = draw_keys(jax.random.fold_in(arg_keys[5], 71), 0)
    values = normal_values(arg_keys[2], (TOKENS, HD), 1.0, 6.0, ((0, 32),))
    grad_out = normal_values(arg_keys[3], (TOKENS, GROUP * HD), 16.0, 96.0, ((0, 32),))
    span_slot = draw_span_slot(jax.random.fold_in(arg_keys[5], 71), 0)
    return dict(queries=queries, keys=keys, values=values, grad_out=grad_out, span_slot=span_slot)


NEG_FILL = -1e+30

def reference(queries, keys, values, grad_out, span_slot):
    tokens = keys.shape[0]
    span_len = tokens // span_slot.shape[0]
    offsets = jnp.arange(span_len, dtype=jnp.int32)
    position = (span_slot[:, None].astype(jnp.int32) * span_len + offsets[None, :]).reshape(-1)
    scale = 1.0 / math.sqrt(HD)
    q_block = math.gcd(tokens, 128)
    blocks = tokens // q_block
    q_all = queries.reshape(blocks, q_block * GROUP, HD)
    do_all = grad_out.reshape(blocks, q_block * GROUP, HD)
    pos_all = jnp.repeat(position, GROUP).reshape(blocks, q_block * GROUP)

    def step(carry, item):
        dkey, dval = carry
        q_rows, do_rows, q_pos = item
        live = q_pos[:, None] >= position[None, :]
        scores = jnp.where(live, jnp.dot(q_rows, keys.T, preferred_element_type=jnp.float32) * scale, NEG_FILL)
        top = lax.optimization_barrier(jnp.max(scores, axis=1))
        lse = top + jnp.log(lax.optimization_barrier(jnp.sum(jnp.where(live, jnp.exp(scores - top[:, None]), 0.0), axis=1)))
        probs = jnp.where(live, jnp.exp(scores - lse[:, None]), 0.0)
        dprobs = jnp.dot(do_rows, values.T, preferred_element_type=jnp.float32)
        delta = lax.optimization_barrier(jnp.sum(probs * dprobs, axis=1))
        dscores = (probs * (dprobs - delta[:, None]) * scale).astype(jnp.bfloat16)
        dq_rows = jnp.dot(dscores, keys, preferred_element_type=jnp.float32).astype(jnp.bfloat16)
        dkey = dkey + jnp.dot(dscores.T, q_rows, preferred_element_type=jnp.float32)
        dval = dval + jnp.dot(probs.astype(jnp.bfloat16).T, do_rows, preferred_element_type=jnp.float32)
        return ((dkey, dval), dq_rows)
    start = (jnp.zeros((tokens, HD), jnp.float32), jnp.zeros((tokens, HD), jnp.float32))
    (dkey, dval), dq_all = lax.scan(step, start, (q_all, do_all, pos_all))
    grad_queries = dq_all.reshape(tokens, GROUP * HD)
    return (grad_queries, dkey.astype(jnp.bfloat16), dval.astype(jnp.bfloat16))
```

```python
import functools
import math

import jax
import jax.numpy as jnp
import numpy as np
from jax import lax
from jax.experimental import pallas as pl
from jax.experimental.pallas import tpu as pltpu
from jax.sharding import PartitionSpec as P

NEG_FILL = -1e30
LOG2E = math.log2(math.e)
MIB = 1024 * 1024
MESH = pl.DeviceIdType.MESH


def bits_of(outer, inner):
    near = [("inner", b) for b in range(inner.bit_length() - 1)]
    chips = [("outer", b) for b in range(1, outer.bit_length() - 1)]
    core = [("outer", 0)]
    return near + chips + core, near + chips[::-1] + core


def place_of(order, o, i):
    place = 0
    for at, (axis, b) in enumerate(order):
        place = place + (((o if axis == "outer" else i) // 2**b) % 2) * 2**at
    return place


def partner_of(axis, b, o, i):
    if axis == "outer":
        return (o + (1 - 2 * ((o // 2**b) % 2)) * 2**b, i)
    return (o, i + (1 - 2 * ((i // 2**b) % 2)) * 2**b)


def greet(order, o, i):
    barrier = pltpu.get_barrier_semaphore()
    for axis, b in order:
        pl.semaphore_signal(barrier, inc=1, device_id=partner_of(axis, b, o, i), device_id_type=MESH)
    pl.semaphore_wait(barrier, len(order))


def gather_kernel(orders, k_in, v_in, k_out, v_out, send, recv):
    o, i = lax.axis_index("outer"), lax.axis_index("inner")
    rows = k_in.shape[0]
    steps = len(orders[0])
    greet(orders[0], o, i)
    places = [place_of(order, o, i) for order in orders]
    for src, out, place in ((k_in, k_out, places[0]), (v_in, v_out, places[1])):
        out[pl.ds(pl.multiple_of(place * rows, rows), rows), :] = src[...]
    copies = {}

    def begin(a, step):
        out = (k_out, v_out)[a]
        size = rows * 2**step
        part = out.at[pl.ds(pl.multiple_of((places[a] // 2**step) * size, size), size), :]
        axis, b = orders[a][step]
        copies[a, step] = pltpu.make_async_remote_copy(
            src_ref=part, dst_ref=part, send_sem=send.at[a, step], recv_sem=recv.at[a, step],
            device_id=partner_of(axis, b, o, i), device_id_type=MESH)
        copies[a, step].start()

    for a in (0, 1):
        begin(a, 0)
    for step in range(steps):
        for a in (0, 1):
            copies[a, step].wait_recv()
            if step + 1 < steps:
                begin(a, step + 1)
    for copy in copies.values():
        copy.wait_send()


def scatter_kernel(orders, k_in, v_in, k_out, v_out, k_acc, v_acc, k_got, v_got, send, recv):
    o, i = lax.axis_index("outer"), lax.axis_index("inner")
    rows = k_out.shape[0]
    steps = len(orders[0])
    half = 2 ** (steps - 1)
    greet(orders[0], o, i)
    places = [place_of(order, o, i) for order in orders]
    ins, outs, accs, gots = (k_in, v_in), (k_out, v_out), (k_acc, v_acc), (k_got, v_got)
    copies = {}

    def spot(place, step, wrap):
        size = rows * 2**step
        return pl.ds(pl.multiple_of(((place % wrap) // 2**step) * size, size), size)

    def begin(a, step):
        place, size = places[a], rows * 2**step
        theirs = place + (1 - 2 * ((place // 2**step) % 2)) * 2**step
        axis, b = orders[a][step]
        src = ins[a].at[spot(theirs, step, 2 * half), :] if step == steps - 1 else accs[a].at[spot(theirs, step, half), :]
        copies[a, step] = pltpu.make_async_remote_copy(
            src_ref=src, dst_ref=gots[a].at[pl.ds(size, size), :],
            send_sem=send.at[a, step], recv_sem=recv.at[a, step],
            device_id=partner_of(axis, b, o, i), device_id_type=MESH)
        copies[a, step].start()

    for a in (0, 1):
        begin(a, steps - 1)
    for step in range(steps - 1, -1, -1):
        size = rows * 2**step
        for a in (0, 1):
            copies[a, step].wait_recv()
            mine = ins[a][spot(places[a], step, 2 * half), :] if step == steps - 1 else accs[a][spot(places[a], step, half), :]
            total = mine.astype(jnp.float32) + gots[a][pl.ds(size, size), :].astype(jnp.float32)
            if step:
                accs[a][spot(places[a], step, half), :] = total.astype(jnp.bfloat16)
                begin(a, step - 1)
            else:
                outs[a][...] = total.astype(jnp.bfloat16)
    for copy in copies.values():
        copy.wait_send()


def attend_kernel(inner, blk_spans, slots, tab_k, tab_v, q_ref, do_ref, k_ref, v_ref,
                  dq_ref, dk_ref, dv_ref, at_k, at_v, ks, vs, dks, dvs):
    spans = slots.shape[0]
    span = q_ref.shape[0] // 2
    hd = k_ref.shape[1]
    group = q_ref.shape[1] // hd
    blk = blk_spans * span
    scale = 1.0 / math.sqrt(hd)
    f32 = jnp.float32
    linear = lax.axis_index("outer") * inner + lax.axis_index("inner")

    def note(j, _):
        s = slots[j]
        at_k[s] = tab_k[j]
        at_v[s] = tab_v[j]
        return 0

    lax.fori_loop(0, spans, note, 0)
    tops = [slots[2 * linear], slots[2 * linear + 1]]
    used = (tops[1] // blk_spans + 1) * blk_spans

    def sort(s, _):
        to = pl.ds(pl.multiple_of(s * span, span), span)
        ks[to, :] = k_ref[pl.ds(pl.multiple_of(at_k[s] * span, span), span), :]
        vs[to, :] = v_ref[pl.ds(pl.multiple_of(at_v[s] * span, span), span), :]
        return 0

    lax.fori_loop(0, used, sort, 0)
    nt = (((1,), (1,)), ((), ()))
    tn = (((0,), (0,)), ((), ()))
    width = group * span

    for g in (1, 0):
        rows = slice(g * span, (g + 1) * span)
        q = jnp.concatenate([q_ref[rows, h * hd:(h + 1) * hd] for h in range(group)], axis=0)
        do = jnp.concatenate([do_ref[rows, h * hd:(h + 1) * hd] for h in range(group)], axis=0)
        last = tops[g] // blk_spans
        lane = lax.broadcasted_iota(jnp.int32, (blk, width), 1) % span
        low = lax.broadcasted_iota(jnp.int32, (blk, width), 0)

        def load(n):
            at = pl.ds(pl.multiple_of(n * blk, blk), blk)
            return at, ks[at, :], vs[at, :]

        def logits(k, n, masked):
            t = lax.dot_general(k, q, nt, preferred_element_type=f32) * (scale * LOG2E)
            if masked:
                t = jnp.where(low + n * blk <= lane + tops[g] * span, t, NEG_FILL)
            return t

        def stats(n, carry, masked):
            top, total, weighted = carry
            _, k, v = load(n)
            t = logits(k, n, masked)
            dp = lax.dot_general(v, do, nt, preferred_element_type=f32)
            new = jnp.maximum(top, jnp.max(t, axis=0, keepdims=True))
            shrink = jnp.exp2(top - new)
            e = jnp.exp2(t - new)
            return (new, total * shrink + jnp.sum(e, axis=0, keepdims=True),
                    weighted * shrink + jnp.sum(e * dp, axis=0, keepdims=True))

        carry = (jnp.full((1, width), NEG_FILL, f32), jnp.zeros((1, width), f32), jnp.zeros((1, width), f32))
        carry = lax.fori_loop(0, last, functools.partial(stats, masked=False), carry)
        top, total, weighted = stats(last, carry, True)
        lse = top + jnp.log2(total)
        delta = weighted / total

        def grads(n, dq, masked):
            at, k, v = load(n)
            p = jnp.exp2(logits(k, n, masked) - lse)
            dp = lax.dot_general(v, do, nt, preferred_element_type=f32)
            ds = (p * (dp - delta) * scale).astype(jnp.bfloat16)
            dk = jnp.dot(ds, q, preferred_element_type=f32)
            dv = jnp.dot(p.astype(jnp.bfloat16), do, preferred_element_type=f32)
            if g == 1:
                dks[at, :] = dk
                dvs[at, :] = dv
            else:
                dks[at, :] += dk
                dvs[at, :] += dv
            return dq + lax.dot_general(k, ds, tn, preferred_element_type=f32)

        dq = lax.fori_loop(0, last, functools.partial(grads, masked=False), jnp.zeros((hd, width), f32))
        dq = grads(last, dq, True).T
        for h in range(group):
            dq_ref[rows, h * hd:(h + 1) * hd] = dq[h * span:(h + 1) * span, :].astype(jnp.bfloat16)

    def place(s, _):
        at = pl.ds(pl.multiple_of(s * span, span), span)
        dk_ref[pl.ds(pl.multiple_of(at_k[s] * span, span), span), :] = dks[at, :].astype(jnp.bfloat16)
        dv_ref[pl.ds(pl.multiple_of(at_v[s] * span, span), span), :] = dvs[at, :].astype(jnp.bfloat16)
        return 0

    def blank(s, _):
        none = jnp.zeros((span, hd), jnp.bfloat16)
        dk_ref[pl.ds(pl.multiple_of(at_k[s] * span, span), span), :] = none
        dv_ref[pl.ds(pl.multiple_of(at_v[s] * span, span), span), :] = none
        return 0

    lax.fori_loop(0, used, place, 0)
    lax.fori_loop(used, spans, blank, 0)


def local(outer, inner, queries, keys, values, grad_out, span_slot):
    rows, hd = keys.shape
    total = rows * outer * inner
    spans = span_slot.shape[0]
    orders = bits_of(outer, inner)
    steps = len(orders[0])
    low = jnp.bfloat16
    vmem, smem = pl.BlockSpec(memory_space=pltpu.VMEM), pl.BlockSpec(memory_space=pltpu.SMEM)
    sems = [pltpu.SemaphoreType.DMA((2, steps)), pltpu.SemaphoreType.DMA((2, steps))]
    whole = jax.ShapeDtypeStruct((total, hd), low)
    block = jax.ShapeDtypeStruct((rows, hd), low)
    keys_all, values_all = pl.pallas_call(
        functools.partial(gather_kernel, orders),
        out_shape=(whole, whole), in_specs=[vmem] * 2, out_specs=(vmem, vmem), scratch_shapes=sems,
        compiler_params=pltpu.CompilerParams(collective_id=0, has_side_effects=True, vmem_limit_bytes=40 * MIB),
    )(keys, values)
    tables = [
        jnp.asarray(np.array([2 * place_of(order, j // 2 // inner, j // 2 % inner) + j % 2 for j in range(spans)], np.int32))
        for order in orders
    ]
    grad_queries, dk, dv = pl.pallas_call(
        functools.partial(attend_kernel, inner, math.gcd(spans, 4)),
        out_shape=(jax.ShapeDtypeStruct(queries.shape, low), whole, whole),
        in_specs=[smem] * 3 + [vmem] * 4, out_specs=(vmem, vmem, vmem),
        scratch_shapes=[pltpu.SMEM((spans,), jnp.int32), pltpu.SMEM((spans,), jnp.int32),
                        pltpu.VMEM((total, hd), low), pltpu.VMEM((total, hd), low),
                        pltpu.VMEM((total, hd), jnp.float32), pltpu.VMEM((total, hd), jnp.float32)],
        compiler_params=pltpu.CompilerParams(vmem_limit_bytes=56 * MIB),
    )(span_slot, *tables, queries, grad_out, keys_all, values_all)
    grad_keys, grad_values = pl.pallas_call(
        functools.partial(scatter_kernel, orders),
        out_shape=(block, block), in_specs=[vmem] * 2, out_specs=(vmem, vmem),
        scratch_shapes=[pltpu.VMEM((total // 2, hd), low), pltpu.VMEM((total // 2, hd), low),
                        pltpu.VMEM((total, hd), low), pltpu.VMEM((total, hd), low)] + sems,
        compiler_params=pltpu.CompilerParams(collective_id=1, has_side_effects=True, vmem_limit_bytes=40 * MIB),
    )(dk, dv)
    return grad_queries, grad_keys, grad_values


def solution(mesh):
    rows = P(("outer", "inner"), None)
    return jax.shard_map(
        functools.partial(local, mesh.shape["outer"], mesh.shape["inner"]),
        mesh=mesh,
        in_specs=(rows, rows, rows, rows, P()),
        out_specs=(rows, rows, rows),
        check_vma=False,
    )
```

```python
import functools
import math

import jax
import jax.numpy as jnp
import numpy as np
from jax import lax
from jax.experimental import pallas as pl
from jax.experimental.pallas import tpu as pltpu
from jax.sharding import PartitionSpec as P

NEG_FILL = -1e30
LOG2E = math.log2(math.e)
MIB = 1024 * 1024
MESH = pl.DeviceIdType.MESH


def bits_of(outer, inner):
    near = [("inner", b) for b in range(inner.bit_length() - 1)]
    chips = [("outer", b) for b in range(1, outer.bit_length() - 1)]
    core = [("outer", 0)]
    return near + chips + core, near[::-1] + chips[::-1] + core


def place_of(order, o, i):
    place = 0
    for at, (axis, b) in enumerate(order):
        place = place + (((o if axis == "outer" else i) // 2**b) % 2) * 2**at
    return place


def partner_of(axis, b, o, i):
    if axis == "outer":
        return (o + (1 - 2 * ((o // 2**b) % 2)) * 2**b, i)
    return (o, i + (1 - 2 * ((i // 2**b) % 2)) * 2**b)


def greet(order, o, i):
    barrier = pltpu.get_barrier_semaphore()
    for axis, b in order:
        pl.semaphore_signal(barrier, inc=1, device_id=partner_of(axis, b, o, i), device_id_type=MESH)
    pl.semaphore_wait(barrier, len(order))


def gather_kernel(orders, k_in, v_in, k_out, v_out, send, recv, own):
    o, i = lax.axis_index("outer"), lax.axis_index("inner")
    rows = k_in.shape[0]
    chain = len(orders[0]) - 1
    near = sum(axis == "inner" for axis, _ in orders[0])
    places = [place_of(order, o, i) for order in orders]
    outs = (k_out, v_out)

    def span_of(place, step):
        size = rows * 2**step
        return pl.ds(pl.multiple_of((place // 2**step) * size, size), size)

    owned = [
        pltpu.make_async_copy((k_in, v_in)[a], outs[a].at[span_of(places[a], 0), :], own.at[a]) for a in (0, 1)
    ]
    for copy in owned:
        copy.start()
    greet(orders[0], o, i)
    copies = {}

    def begin(a, name, part, bit):
        part = outs[a].at[part, :]
        copies[a, name] = pltpu.make_async_remote_copy(
            src_ref=part, dst_ref=part, send_sem=send.at[a, name], recv_sem=recv.at[a, name],
            device_id=partner_of(*bit, o, i), device_id_type=MESH)
        copies[a, name].start()

    for a in (0, 1):
        owned[a].wait()
        begin(a, 0, span_of(places[a], 0), orders[a][0])
    core = orders[0][chain]
    for step in range(chain):
        for a in (0, 1):
            copies[a, step].wait_recv()
            if step + 1 < chain:
                begin(a, step + 1, span_of(places[a], step + 1), orders[a][step + 1])
            if step == near - 1:
                begin(a, chain, span_of(places[a], near), core)
            elif step >= near:
                theirs = places[a] + (1 - 2 * ((places[a] // 2**step) % 2)) * 2**step
                begin(a, chain + 1 + step - near, span_of(theirs, step), core)
    for (_, name), copy in copies.items():
        copy.wait_send()
        if name >= chain:
            copy.wait_recv()


def scatter_kernel(orders, k_in, v_in, k_out, v_out, k_acc, v_acc, k_got, v_got, k_core, v_core, send, recv):
    o, i = lax.axis_index("outer"), lax.axis_index("inner")
    rows = k_out.shape[0]
    chain = len(orders[0]) - 1
    near = sum(axis == "inner" for axis, _ in orders[0])
    greet(orders[0], o, i)
    half = 2**chain
    ins, outs, accs = (k_in, v_in), (k_out, v_out), (k_acc, v_acc)
    gots, cores = (k_got, v_got), (k_core, v_core)
    full = [place_of(order, o, i) for order in orders]
    places = [place % half for place in full]
    sides = [place // half for place in full]
    copies = {}

    def spot(place, step):
        size = rows * 2**step
        return pl.ds(pl.multiple_of((place // 2**step) * size, size), size)

    def inside(place, step, side):
        size = rows * 2**step
        return pl.ds(pl.multiple_of((place // 2**step) * size + side * half * rows, size), size)

    def theirs(a, step):
        return places[a] + (1 - 2 * ((places[a] // 2**step) % 2)) * 2**step

    def begin(a, name, src, dst, bit):
        copies[a, name] = pltpu.make_async_remote_copy(
            src_ref=src, dst_ref=dst, send_sem=send.at[a, name], recv_sem=recv.at[a, name],
            device_id=partner_of(*bit, o, i), device_id_type=MESH)
        copies[a, name].start()

    def forward(a, step):
        size = rows * 2**step
        begin(a, step, accs[a].at[spot(theirs(a, step), step), :], gots[a].at[pl.ds(size, size), :], orders[a][step])

    def pieces(a):
        return [(chain + 1 + step - near, theirs(a, step), step) for step in range(chain - 1, near - 1, -1)] + [
            (chain, places[a], near)]

    def join(a, which):
        name, place, step = pieces(a)[which]
        copies[a, name].wait_recv()
        at = spot(place, step)
        total = ins[a][inside(place, step, sides[a]), :].astype(jnp.float32) + cores[a][at, :].astype(jnp.float32)
        accs[a][at, :] = total.astype(jnp.bfloat16)

    chips = chain - near
    for which in range(chips + 1):
        for a in (0, 1):
            name, place, step = pieces(a)[which]
            begin(a, name, ins[a].at[inside(place, step, 1 - sides[a]), :], cores[a].at[spot(place, step), :],
                  orders[a][chain])
    for a in (0, 1):
        join(a, 0)
        forward(a, chain - 1)
    for which in range(1, chips + 1):
        for a in (0, 1):
            join(a, which)
    for step in range(chain - 1, -1, -1):
        size = rows * 2**step
        for a in (0, 1):
            copies[a, step].wait_recv()

            def add(part, place, at_step):
                lo = (place // 2**at_step) * 2**at_step - (places[a] // 2**step) * 2**step
                got = gots[a][pl.ds(pl.multiple_of(size + lo * rows, rows), rows * 2**at_step), :]
                return accs[a][part, :].astype(jnp.float32) + got.astype(jnp.float32)

            if step:
                first, rest = spot(theirs(a, step - 1), step - 1), spot(places[a], step - 1)
                accs[a][first, :] = add(first, theirs(a, step - 1), step - 1).astype(jnp.bfloat16)
                forward(a, step - 1)
                accs[a][rest, :] = add(rest, places[a], step - 1).astype(jnp.bfloat16)
            else:
                outs[a][...] = add(spot(places[a], 0), places[a], 0).astype(jnp.bfloat16)
    for copy in copies.values():
        copy.wait_send()


def attend_kernel(inner, blk_spans, slots, tab_k, tab_v, q_in, do_in, k_ref, v_ref,
                  dq_ref, dk_ref, dv_ref, at_k, at_v, ks, vs, q_ref, do_ref, sem):
    fetches = [pltpu.make_async_copy(q_in, q_ref, sem.at[0]), pltpu.make_async_copy(do_in, do_ref, sem.at[1])]
    for fetch in fetches:
        fetch.start()
    spans = slots.shape[0]
    span = q_ref.shape[0] // 2
    hd = k_ref.shape[1]
    group = q_ref.shape[1] // hd
    blk = blk_spans * span
    scale = 1.0 / math.sqrt(hd)
    f32 = jnp.float32
    linear = lax.axis_index("outer") * inner + lax.axis_index("inner")

    def note(j, _):
        s = slots[j]
        at_k[s] = tab_k[j] * span
        at_v[s] = tab_v[j] * span
        return 0

    lax.fori_loop(0, spans, note, 0)
    tops = [slots[2 * linear], slots[2 * linear + 1]]
    lasts = [top // blk_spans for top in tops]

    def rows_at(table, s):
        return pl.ds(pl.multiple_of(table[s], span), span)

    nt = (((1,), (1,)), ((), ()))
    tn = (((0,), (0,)), ((), ()))
    width = group * span

    def stack(ref):
        return jnp.concatenate(
            [ref[g * span:(g + 1) * span, h * hd:(h + 1) * hd] for g in (0, 1) for h in range(group)], axis=0)

    for fetch in fetches:
        fetch.wait()
    q, do = stack(q_ref), stack(do_ref)
    lane = lax.broadcasted_iota(jnp.int32, (1, 2 * width), 1)
    q_pos = lane % span + jnp.where(lane < width, tops[0], tops[1]) * span
    low = lax.broadcasted_iota(jnp.int32, (blk, 1), 0)

    def logits(k, n, first, masked):
        t = lax.dot_general(k, q[first:], nt, preferred_element_type=f32) * (scale * LOG2E)
        if masked:
            t = jnp.where(low + n * blk <= q_pos[:, first:], t, NEG_FILL)
        return t

    def stats(n, carry, first, masked):
        top, total, weighted = carry
        at = pl.ds(pl.multiple_of(n * blk, blk), blk)
        spots = [(n * blk_spans + j) for j in range(blk_spans)]
        k = jnp.concatenate([k_ref[rows_at(at_k, s), :] for s in spots], axis=0)
        v = jnp.concatenate([v_ref[rows_at(at_v, s), :] for s in spots], axis=0)
        ks[at, :] = k
        vs[at, :] = v
        t = logits(k, n, first, masked)
        dp = lax.dot_general(v, do[first:], nt, preferred_element_type=f32)
        new = jnp.maximum(top, jnp.max(t, axis=0, keepdims=True))
        shrink = jnp.exp2(top - new)
        e = jnp.exp2(t - new)
        return (new, total * shrink + jnp.sum(e, axis=0, keepdims=True),
                weighted * shrink + jnp.sum(e * dp, axis=0, keepdims=True))

    def sweep(step, carry, narrow):
        carry = lax.fori_loop(0, lasts[0], functools.partial(step, first=0, masked=False), carry)
        carry = step(lasts[0], carry, 0, True)
        late = narrow(carry)
        late = lax.fori_loop(lasts[0] + 1, lasts[1], functools.partial(step, first=width, masked=False), late)
        return carry, step(lasts[1], late, width, True)

    start = (jnp.full((1, 2 * width), NEG_FILL, f32), jnp.zeros((1, 2 * width), f32), jnp.zeros((1, 2 * width), f32))
    early, late = sweep(stats, start, lambda carry: tuple(x[:, width:] for x in carry))
    top, total, weighted = [jnp.concatenate([x[:, :width], y], axis=1) for x, y in zip(early, late)]
    lse = top + jnp.log2(total)
    delta = weighted / total

    def grads(n, dq, first, masked):
        at = pl.ds(pl.multiple_of(n * blk, blk), blk)
        k, v = ks[at, :], vs[at, :]
        p = jnp.exp2(logits(k, n, first, masked) - lse[:, first:])
        dp = lax.dot_general(v, do[first:], nt, preferred_element_type=f32)
        ds = (p * (dp - delta[:, first:]) * scale).astype(jnp.bfloat16)
        dk = jnp.dot(ds, q[first:], preferred_element_type=f32).astype(jnp.bfloat16)
        dv = jnp.dot(p.astype(jnp.bfloat16), do[first:], preferred_element_type=f32).astype(jnp.bfloat16)
        for j in range(blk_spans):
            s = n * blk_spans + j
            dk_ref[rows_at(at_k, s), :] = dk[j * span:(j + 1) * span]
            dv_ref[rows_at(at_v, s), :] = dv[j * span:(j + 1) * span]
        return dq + lax.dot_general(k, ds, tn, preferred_element_type=f32)

    early, late = sweep(grads, jnp.zeros((hd, 2 * width), f32), lambda dq: dq[:, width:])
    dq = jnp.concatenate([early[:, :width], late], axis=1).T
    for g in (0, 1):
        for h in range(group):
            at = (g * group + h) * span
            dq_ref[g * span:(g + 1) * span, h * hd:(h + 1) * hd] = dq[at:at + span].astype(jnp.bfloat16)

    def blank(s, _):
        none = jnp.zeros((span, hd), jnp.bfloat16)
        dk_ref[rows_at(at_k, s), :] = none
        dv_ref[rows_at(at_v, s), :] = none
        return 0

    lax.fori_loop((lasts[1] + 1) * blk_spans, spans, blank, 0)


def local(outer, inner, queries, keys, values, grad_out, span_slot):
    rows, hd = keys.shape
    total = rows * outer * inner
    spans = span_slot.shape[0]
    orders = bits_of(outer, inner)
    steps = len(orders[0])
    low = jnp.bfloat16
    vmem, smem = pl.BlockSpec(memory_space=pltpu.VMEM), pl.BlockSpec(memory_space=pltpu.SMEM)
    moves = steps + outer.bit_length() - 2
    hbm = pl.BlockSpec(memory_space=pltpu.HBM)
    sems = [pltpu.SemaphoreType.DMA((2, moves)), pltpu.SemaphoreType.DMA((2, moves))]
    unit = total * hd
    whole = jax.ShapeDtypeStruct((total, hd), low)
    block = jax.ShapeDtypeStruct((rows, hd), low)
    keys_all, values_all = pl.pallas_call(
        functools.partial(gather_kernel, orders),
        out_shape=(whole, whole), in_specs=[hbm] * 2, out_specs=(vmem, vmem),
        scratch_shapes=sems + [pltpu.SemaphoreType.DMA((2,))],
        compiler_params=pltpu.CompilerParams(
            collective_id=0, has_side_effects=True, vmem_limit_bytes=4 * unit + 4 * MIB),
    )(keys, values)
    tables = [
        jnp.asarray(np.array([2 * place_of(order, j // 2 // inner, j // 2 % inner) + j % 2 for j in range(spans)], np.int32))
        for order in orders
    ]
    grad_queries, dk, dv = pl.pallas_call(
        functools.partial(attend_kernel, inner, math.gcd(spans, 4)),
        out_shape=(jax.ShapeDtypeStruct(queries.shape, low), whole, whole),
        in_specs=[smem] * 3 + [hbm] * 2 + [vmem] * 2, out_specs=(vmem, vmem, vmem),
        scratch_shapes=[pltpu.SMEM((spans,), jnp.int32), pltpu.SMEM((spans,), jnp.int32),
                        pltpu.VMEM((total, hd), low), pltpu.VMEM((total, hd), low),
                        pltpu.VMEM(queries.shape, low), pltpu.VMEM(queries.shape, low),
                        pltpu.SemaphoreType.DMA((2,))],
        compiler_params=pltpu.CompilerParams(vmem_limit_bytes=12 * unit + 12 * MIB),
    )(span_slot, *tables, queries, grad_out, keys_all, values_all)
    grad_keys, grad_values = pl.pallas_call(
        functools.partial(scatter_kernel, orders),
        out_shape=(block, block), in_specs=[vmem] * 2, out_specs=(vmem, vmem),
        scratch_shapes=[pltpu.VMEM((total // 2, hd), low), pltpu.VMEM((total // 2, hd), low),
                        pltpu.VMEM((total // 2, hd), low), pltpu.VMEM((total // 2, hd), low),
                        pltpu.VMEM((total // 2, hd), low), pltpu.VMEM((total // 2, hd), low)] + sems,
        compiler_params=pltpu.CompilerParams(
            collective_id=1, has_side_effects=True, vmem_limit_bytes=10 * unit + 4 * MIB),
    )(dk, dv)
    return grad_queries, grad_keys, grad_values


def solution(mesh):
    rows = P(("outer", "inner"), None)
    return jax.shard_map(
        functools.partial(local, mesh.shape["outer"], mesh.shape["inner"]),
        mesh=mesh,
        in_specs=(rows, rows, rows, rows, P()),
        out_specs=(rows, rows, rows),
        check_vma=False,
    )
```

```python
import functools
import math

import jax
import jax.numpy as jnp
import numpy as np
from jax import lax
from jax.experimental import pallas as pl
from jax.experimental.pallas import tpu as pltpu
from jax.sharding import PartitionSpec as P

NEG_FILL = -1e30
LOG2E = math.log2(math.e)
MIB = 1024 * 1024
MESH = pl.DeviceIdType.MESH


def bits_of(outer, inner):
    near = [("inner", b) for b in range(inner.bit_length() - 1)]
    chips = [("outer", b) for b in range(1, outer.bit_length() - 1)]
    core = [("outer", 0)]
    return near + chips + core, near[::-1] + chips[::-1] + core


def place_of(order, o, i):
    place = 0
    for at, (axis, b) in enumerate(order):
        place = place + (((o if axis == "outer" else i) // 2**b) % 2) * 2**at
    return place


def partner_of(axis, b, o, i):
    if axis == "outer":
        return (o + (1 - 2 * ((o // 2**b) % 2)) * 2**b, i)
    return (o, i + (1 - 2 * ((i // 2**b) % 2)) * 2**b)


def greet(order, o, i):
    barrier = pltpu.get_barrier_semaphore()
    for axis, b in order:
        pl.semaphore_signal(barrier, inc=1, device_id=partner_of(axis, b, o, i), device_id_type=MESH)
    pl.semaphore_wait(barrier, len(order))


def gather_kernel(orders, k_in, v_in, k_out, v_out, send, recv, own):
    o, i = lax.axis_index("outer"), lax.axis_index("inner")
    rows = k_in.shape[0]
    chain = len(orders[0]) - 1
    near = sum(axis == "inner" for axis, _ in orders[0])
    places = [place_of(order, o, i) for order in orders]
    outs = (k_out, v_out)

    def span_of(place, step):
        size = rows * 2**step
        return pl.ds(pl.multiple_of((place // 2**step) * size, size), size)

    owned = [
        pltpu.make_async_copy((k_in, v_in)[a], outs[a].at[span_of(places[a], 0), :], own.at[a]) for a in (0, 1)
    ]
    for copy in owned:
        copy.start()
    greet(orders[0], o, i)
    copies = {}

    def begin(a, name, part, bit):
        part = outs[a].at[part, :]
        copies[a, name] = pltpu.make_async_remote_copy(
            src_ref=part, dst_ref=part, send_sem=send.at[a, name], recv_sem=recv.at[a, name],
            device_id=partner_of(*bit, o, i), device_id_type=MESH)
        copies[a, name].start()

    for a in (0, 1):
        owned[a].wait()
        begin(a, 0, span_of(places[a], 0), orders[a][0])
    core = orders[0][chain]
    for step in range(chain):
        for a in (0, 1):
            copies[a, step].wait_recv()
            if step + 1 < chain:
                begin(a, step + 1, span_of(places[a], step + 1), orders[a][step + 1])
            if step == near - 1:
                begin(a, chain, span_of(places[a], near), core)
            elif step >= near:
                theirs = places[a] + (1 - 2 * ((places[a] // 2**step) % 2)) * 2**step
                begin(a, chain + 1 + step - near, span_of(theirs, step), core)
    for (_, name), copy in copies.items():
        copy.wait_send()
        if name >= chain:
            copy.wait_recv()


def scatter_kernel(orders, k_in, v_in, k_out, v_out, k_acc, v_acc, k_got, v_got, k_core, v_core, send, recv):
    o, i = lax.axis_index("outer"), lax.axis_index("inner")
    rows = k_out.shape[0]
    chain = len(orders[0]) - 1
    near = sum(axis == "inner" for axis, _ in orders[0])
    greet(orders[0], o, i)
    half = 2**chain
    ins, outs, accs = (k_in, v_in), (k_out, v_out), (k_acc, v_acc)
    gots, cores = (k_got, v_got), (k_core, v_core)
    full = [place_of(order, o, i) for order in orders]
    places = [place % half for place in full]
    sides = [place // half for place in full]
    copies = {}

    def spot(place, step):
        size = rows * 2**step
        return pl.ds(pl.multiple_of((place // 2**step) * size, size), size)

    def inside(place, step, side):
        size = rows * 2**step
        return pl.ds(pl.multiple_of((place // 2**step) * size + side * half * rows, size), size)

    def theirs(a, step):
        return places[a] + (1 - 2 * ((places[a] // 2**step) % 2)) * 2**step

    def begin(a, name, src, dst, bit):
        copies[a, name] = pltpu.make_async_remote_copy(
            src_ref=src, dst_ref=dst, send_sem=send.at[a, name], recv_sem=recv.at[a, name],
            device_id=partner_of(*bit, o, i), device_id_type=MESH)
        copies[a, name].start()

    def forward(a, step):
        size = rows * 2**step
        begin(a, step, accs[a].at[spot(theirs(a, step), step), :], gots[a].at[pl.ds(size, size), :], orders[a][step])

    def pieces(a):
        return [(chain + 1 + step - near, theirs(a, step), step) for step in range(chain - 1, near - 1, -1)] + [
            (chain, places[a], near)]

    def join(a, which):
        name, place, step = pieces(a)[which]
        copies[a, name].wait_recv()
        at = spot(place, step)
        total = ins[a][inside(place, step, sides[a]), :].astype(jnp.float32) + cores[a][at, :].astype(jnp.float32)
        accs[a][at, :] = total.astype(jnp.bfloat16)

    chips = chain - near
    for which in range(chips + 1):
        for a in (0, 1):
            name, place, step = pieces(a)[which]
            begin(a, name, ins[a].at[inside(place, step, 1 - sides[a]), :], cores[a].at[spot(place, step), :],
                  orders[a][chain])
    for a in (0, 1):
        join(a, 0)
        forward(a, chain - 1)
    for which in range(1, chips + 1):
        for a in (0, 1):
            join(a, which)
    for step in range(chain - 1, -1, -1):
        size = rows * 2**step
        for a in (0, 1):
            copies[a, step].wait_recv()

            def add(part, place, at_step):
                lo = (place // 2**at_step) * 2**at_step - (places[a] // 2**step) * 2**step
                got = gots[a][pl.ds(pl.multiple_of(size + lo * rows, rows), rows * 2**at_step), :]
                return accs[a][part, :].astype(jnp.float32) + got.astype(jnp.float32)

            if step:
                first, rest = spot(theirs(a, step - 1), step - 1), spot(places[a], step - 1)
                accs[a][first, :] = add(first, theirs(a, step - 1), step - 1).astype(jnp.bfloat16)
                forward(a, step - 1)
                accs[a][rest, :] = add(rest, places[a], step - 1).astype(jnp.bfloat16)
            else:
                outs[a][...] = add(spot(places[a], 0), places[a], 0).astype(jnp.bfloat16)
    for copy in copies.values():
        copy.wait_send()


def attend_kernel(inner, blk_spans, slots, tab_k, tab_v, q_in, do_in, k_ref, v_ref,
                  dq_ref, dk_ref, dv_ref, at_k, at_v, ks, vs, q_ref, do_ref, sem, *kept):
    fetches = [pltpu.make_async_copy(q_in, q_ref, sem.at[0]), pltpu.make_async_copy(do_in, do_ref, sem.at[1])]
    for fetch in fetches:
        fetch.start()
    spans = slots.shape[0]
    span = q_ref.shape[0] // 2
    hd = k_ref.shape[1]
    group = q_ref.shape[1] // hd
    blk = blk_spans * span
    scale = 1.0 / math.sqrt(hd)
    f32 = jnp.float32
    linear = lax.axis_index("outer") * inner + lax.axis_index("inner")

    def note(j, _):
        s = slots[j]
        at_k[s] = tab_k[j] * span
        at_v[s] = tab_v[j] * span
        return 0

    lax.fori_loop(0, spans, note, 0)
    tops = [slots[2 * linear], slots[2 * linear + 1]]
    lasts = [top // blk_spans for top in tops]

    def rows_at(table, s):
        return pl.ds(pl.multiple_of(table[s], span), span)

    nt = (((1,), (1,)), ((), ()))
    tn = (((0,), (0,)), ((), ()))
    width = group * span

    def stack(ref):
        return jnp.concatenate(
            [ref[g * span:(g + 1) * span, h * hd:(h + 1) * hd] for g in (0, 1) for h in range(group)], axis=0)

    for fetch in fetches:
        fetch.wait()
    q, do = stack(q_ref), stack(do_ref)
    lane = lax.broadcasted_iota(jnp.int32, (1, 2 * width), 1)
    q_pos = lane % span + jnp.where(lane < width, tops[0], tops[1]) * span
    low = lax.broadcasted_iota(jnp.int32, (blk, 1), 0)

    def logits(k, n, first, masked):
        t = lax.dot_general(k, q[first:], nt, preferred_element_type=f32) * (scale * LOG2E)
        if masked:
            t = jnp.where(low + n * blk <= q_pos[:, first:], t, NEG_FILL)
        return t

    def stats(n, carry, first, masked):
        top, total, weighted = carry
        at = pl.ds(pl.multiple_of(n * blk, blk), blk)
        spots = [(n * blk_spans + j) for j in range(blk_spans)]
        k = jnp.concatenate([k_ref[rows_at(at_k, s), :] for s in spots], axis=0)
        v = jnp.concatenate([v_ref[rows_at(at_v, s), :] for s in spots], axis=0)
        ks[at, :] = k
        vs[at, :] = v
        t = logits(k, n, first, masked)
        dp = lax.dot_general(v, do[first:], nt, preferred_element_type=f32)
        new = jnp.maximum(top, jnp.max(t, axis=0, keepdims=True))
        shrink = jnp.exp2(top - new)
        e = jnp.exp2(t - new)
        if kept:
            kept[0][at, first:] = e
            kept[1][at, first:] = dp
            kept[2][n, :, first:] = new
        return (new, total * shrink + jnp.sum(e, axis=0, keepdims=True),
                weighted * shrink + jnp.sum(e * dp, axis=0, keepdims=True))

    def sweep(step, carry, narrow):
        carry = lax.fori_loop(0, lasts[0], functools.partial(step, first=0, masked=False), carry)
        carry = step(lasts[0], carry, 0, True)
        late = narrow(carry)
        late = lax.fori_loop(lasts[0] + 1, lasts[1], functools.partial(step, first=width, masked=False), late)
        return carry, step(lasts[1], late, width, True)

    start = (jnp.full((1, 2 * width), NEG_FILL, f32), jnp.zeros((1, 2 * width), f32), jnp.zeros((1, 2 * width), f32))
    early, late = sweep(stats, start, lambda carry: tuple(x[:, width:] for x in carry))
    top, total, weighted = [jnp.concatenate([x[:, :width], y], axis=1) for x, y in zip(early, late)]
    lse = top + jnp.log2(total)
    delta = weighted / total

    def grads(n, dq, first, masked):
        at = pl.ds(pl.multiple_of(n * blk, blk), blk)
        k, v = ks[at, :], vs[at, :]
        if kept:
            p = kept[0][at, first:] * jnp.exp2(kept[2][n, :, first:] - lse[:, first:])
            dp = kept[1][at, first:]
        else:
            p = jnp.exp2(logits(k, n, first, masked) - lse[:, first:])
            dp = lax.dot_general(v, do[first:], nt, preferred_element_type=f32)
        ds = (p * (dp - delta[:, first:]) * scale).astype(jnp.bfloat16)
        dk = jnp.dot(ds, q[first:], preferred_element_type=f32).astype(jnp.bfloat16)
        dv = jnp.dot(p.astype(jnp.bfloat16), do[first:], preferred_element_type=f32).astype(jnp.bfloat16)
        for j in range(blk_spans):
            s = n * blk_spans + j
            dk_ref[rows_at(at_k, s), :] = dk[j * span:(j + 1) * span]
            dv_ref[rows_at(at_v, s), :] = dv[j * span:(j + 1) * span]
        return dq + lax.dot_general(k, ds, tn, preferred_element_type=f32)

    early, late = sweep(grads, jnp.zeros((hd, 2 * width), f32), lambda dq: dq[:, width:])
    dq = jnp.concatenate([early[:, :width], late], axis=1).T
    for g in (0, 1):
        for h in range(group):
            at = (g * group + h) * span
            dq_ref[g * span:(g + 1) * span, h * hd:(h + 1) * hd] = dq[at:at + span].astype(jnp.bfloat16)

    def blank(s, _):
        none = jnp.zeros((span, hd), jnp.bfloat16)
        dk_ref[rows_at(at_k, s), :] = none
        dv_ref[rows_at(at_v, s), :] = none
        return 0

    lax.fori_loop((lasts[1] + 1) * blk_spans, spans, blank, 0)


def local(outer, inner, queries, keys, values, grad_out, span_slot):
    rows, hd = keys.shape
    total = rows * outer * inner
    spans = span_slot.shape[0]
    orders = bits_of(outer, inner)
    steps = len(orders[0])
    low = jnp.bfloat16
    vmem, smem = pl.BlockSpec(memory_space=pltpu.VMEM), pl.BlockSpec(memory_space=pltpu.SMEM)
    moves = steps + outer.bit_length() - 2
    hbm = pl.BlockSpec(memory_space=pltpu.HBM)
    sems = [pltpu.SemaphoreType.DMA((2, moves)), pltpu.SemaphoreType.DMA((2, moves))]
    unit = total * hd
    whole = jax.ShapeDtypeStruct((total, hd), low)
    block = jax.ShapeDtypeStruct((rows, hd), low)
    keys_all, values_all = pl.pallas_call(
        functools.partial(gather_kernel, orders),
        out_shape=(whole, whole), in_specs=[hbm] * 2, out_specs=(vmem, vmem),
        scratch_shapes=sems + [pltpu.SemaphoreType.DMA((2,))],
        compiler_params=pltpu.CompilerParams(
            collective_id=0, has_side_effects=True, vmem_limit_bytes=4 * unit + 4 * MIB),
    )(keys, values)
    tables = [
        jnp.asarray(np.array([2 * place_of(order, j // 2 // inner, j // 2 % inner) + j % 2 for j in range(spans)], np.int32))
        for order in orders
    ]
    blk_spans = math.gcd(spans, 4)
    lanes = rows * queries.shape[1] // hd
    kept = []
    if 8 * total * lanes <= 32 * MIB:
        kept = [pltpu.VMEM((total, lanes), jnp.float32), pltpu.VMEM((total, lanes), jnp.float32),
                pltpu.VMEM((spans // blk_spans, 1, lanes), jnp.float32)]
    grad_queries, dk, dv = pl.pallas_call(
        functools.partial(attend_kernel, inner, blk_spans),
        out_shape=(jax.ShapeDtypeStruct(queries.shape, low), whole, whole),
        in_specs=[smem] * 3 + [hbm] * 2 + [vmem] * 2, out_specs=(vmem, vmem, vmem),
        scratch_shapes=[pltpu.SMEM((spans,), jnp.int32), pltpu.SMEM((spans,), jnp.int32),
                        pltpu.VMEM((total, hd), low), pltpu.VMEM((total, hd), low),
                        pltpu.VMEM(queries.shape, low), pltpu.VMEM(queries.shape, low),
                        pltpu.SemaphoreType.DMA((2,))] + kept,
        compiler_params=pltpu.CompilerParams(
            vmem_limit_bytes=12 * unit + 12 * MIB + (9 * total * lanes if kept else 0)),
    )(span_slot, *tables, queries, grad_out, keys_all, values_all)
    grad_keys, grad_values = pl.pallas_call(
        functools.partial(scatter_kernel, orders),
        out_shape=(block, block), in_specs=[vmem] * 2, out_specs=(vmem, vmem),
        scratch_shapes=[pltpu.VMEM((total // 2, hd), low), pltpu.VMEM((total // 2, hd), low),
                        pltpu.VMEM((total // 2, hd), low), pltpu.VMEM((total // 2, hd), low),
                        pltpu.VMEM((total // 2, hd), low), pltpu.VMEM((total // 2, hd), low)] + sems,
        compiler_params=pltpu.CompilerParams(
            collective_id=1, has_side_effects=True, vmem_limit_bytes=10 * unit + 4 * MIB),
    )(dk, dv)
    return grad_queries, grad_keys, grad_values


def solution(mesh):
    rows = P(("outer", "inner"), None)
    return jax.shard_map(
        functools.partial(local, mesh.shape["outer"], mesh.shape["inner"]),
        mesh=mesh,
        in_specs=(rows, rows, rows, rows, P()),
        out_specs=(rows, rows, rows),
        check_vma=False,
    )
```

```python
import functools
import math

import jax
import jax.numpy as jnp
import numpy as np
from jax import lax
from jax.experimental import pallas as pl
from jax.experimental.pallas import tpu as pltpu
from jax.sharding import PartitionSpec as P

NEG_FILL = -1e30
LOG2E = math.log2(math.e)
MIB = 1024 * 1024
MESH = pl.DeviceIdType.MESH


def bits_of(outer, inner):
    near = [("inner", b) for b in range(inner.bit_length() - 1)]
    chips = [("outer", b) for b in range(1, outer.bit_length() - 1)]
    core = [("outer", 0)]
    return near + chips + core, near[::-1] + chips[::-1] + core


def place_of(order, o, i):
    place = 0
    for at, (axis, b) in enumerate(order):
        place = place + (((o if axis == "outer" else i) // 2**b) % 2) * 2**at
    return place


def partner_of(axis, b, o, i):
    if axis == "outer":
        return (o + (1 - 2 * ((o // 2**b) % 2)) * 2**b, i)
    return (o, i + (1 - 2 * ((i // 2**b) % 2)) * 2**b)


def greet(order, o, i):
    barrier = pltpu.get_barrier_semaphore()
    for axis, b in order:
        pl.semaphore_signal(barrier, inc=1, device_id=partner_of(axis, b, o, i), device_id_type=MESH)
    pl.semaphore_wait(barrier, len(order))


def flip(place, step):
    return place + (1 - 2 * ((place // 2**step) % 2)) * 2**step


def units(place, near):
    return [(place, 0)] + [(flip(place, step), step) for step in range(near)]


def lines(place, near, step):
    if step == near:
        return [place]
    return lines(flip(place, step - 1), near, step - 1) + lines(place, near, step - 1)


def moves_of(near, chips):
    return near + (near + 1) * (2**chips - 1) + chips + 1


def gather_kernel(orders, k_in, v_in, k_out, v_out, send, recv, own):
    o, i = lax.axis_index("outer"), lax.axis_index("inner")
    rows = k_in.shape[0]
    chain = len(orders[0]) - 1
    near = sum(axis == "inner" for axis, _ in orders[0])
    places = [place_of(order, o, i) for order in orders]
    outs = (k_out, v_out)

    def span_of(place, step):
        size = rows * 2**step
        return pl.ds(pl.multiple_of((place // 2**step) * size, size), size)

    owned = [
        pltpu.make_async_copy((k_in, v_in)[a], outs[a].at[span_of(places[a], 0), :], own.at[a]) for a in (0, 1)
    ]
    for copy in owned:
        copy.start()
    greet(orders[0], o, i)
    copies, waited = ({}, {}), set()

    def begin(a, name, part, bit):
        part = outs[a].at[part, :]
        at = len(copies[a])
        copies[a][name] = pltpu.make_async_remote_copy(
            src_ref=part, dst_ref=part, send_sem=send.at[a, at], recv_sem=recv.at[a, at],
            device_id=partner_of(*bit, o, i), device_id_type=MESH)
        copies[a][name].start()

    def arrive(a, name):
        copies[a][name].wait_recv()
        waited.add((a, name))

    def spread(a, path, unit, step):
        place = places[a]
        for bit in path:
            place = flip(place, bit)
        where, size = units(place, near)[unit]
        for later in range(step, chain):
            begin(a, (path + (later,), unit), span_of(where, size), orders[a][later])

    paths = [()]
    for bit in range(near, chain):
        paths = paths + [path + (bit,) for path in paths]
    for a in (0, 1):
        owned[a].wait()
        begin(a, 0, span_of(places[a], 0), orders[a][0])
    for a in (0, 1):
        spread(a, (), 0, near)
    for unit in range(near + 1):
        if unit:
            for a in (0, 1):
                arrive(a, unit - 1)
                if unit < near:
                    begin(a, unit, span_of(places[a], unit), orders[a][unit])
                spread(a, (), unit, near)
                if unit == near:
                    begin(a, "core", span_of(places[a], near), orders[a][chain])
        for path in paths[1:]:
            if path[-1] < chain - 1:
                for a in (0, 1):
                    arrive(a, (path, unit))
                    spread(a, path, unit, path[-1] + 1)
    for bit in range(near, chain):
        for a in (0, 1):
            for unit in range(near + 1):
                for path in paths[1:]:
                    if path[-1] == bit and (a, (path, unit)) not in waited:
                        arrive(a, (path, unit))
            begin(a, ("core", bit), span_of(flip(places[a], bit), bit), orders[a][chain])
    for a in (0, 1):
        for name, copy in copies[a].items():
            copy.wait_send()
            if (a, name) not in waited:
                copy.wait_recv()


def scatter_kernel(orders, k_in, v_in, k_out, v_out, k_acc, v_acc, k_got, v_got, k_core, v_core, send, recv):
    o, i = lax.axis_index("outer"), lax.axis_index("inner")
    rows = k_out.shape[0]
    chain = len(orders[0]) - 1
    near = sum(axis == "inner" for axis, _ in orders[0])
    greet(orders[0], o, i)
    half = 2**chain
    ins, outs, accs = (k_in, v_in), (k_out, v_out), (k_acc, v_acc)
    gots, cores = (k_got, v_got), (k_core, v_core)
    full = [place_of(order, o, i) for order in orders]
    places = [place % half for place in full]
    sides = [place // half for place in full]
    copies = ({}, {})

    def spot(place, step, offset=0):
        size = rows * 2**step
        return pl.ds(pl.multiple_of((place // 2**step) * size + offset, size), size)

    def begin(a, name, src, dst, bit):
        at = len(copies[a])
        copies[a][name] = pltpu.make_async_remote_copy(
            src_ref=src, dst_ref=dst, send_sem=send.at[a, at], recv_sem=recv.at[a, at],
            device_id=partner_of(*bit, o, i), device_id_type=MESH)
        copies[a][name].start()

    def landing(step, place, size):
        return spot(place % 2**step, size, rows * 2**step)

    def forward(a, step, name, place, size):
        begin(a, (step,) + name, accs[a].at[spot(place, size), :], gots[a].at[landing(step, place, size), :],
              orders[a][step])

    def add(a, step, place, size):
        got = gots[a][landing(step, place, size), :]
        return accs[a][spot(place, size), :].astype(jnp.float32) + got.astype(jnp.float32)

    def pieces(a):
        return [(flip(places[a], step), step) for step in range(chain - 1, near - 1, -1)] + [(places[a], near)]

    def join(a, which):
        place, step = pieces(a)[which]
        copies[a]["core", which].wait_recv()
        mine = ins[a][spot(place, step, sides[a] * half * rows), :]
        total = mine.astype(jnp.float32) + cores[a][spot(place, step), :].astype(jnp.float32)
        accs[a][spot(place, step), :] = total.astype(jnp.bfloat16)

    for which in range(chain - near + 1):
        for a in (0, 1):
            place, step = pieces(a)[which]
            begin(a, ("core", which), ins[a].at[spot(place, step, (1 - sides[a]) * half * rows), :],
                  cores[a].at[spot(place, step), :], orders[a][chain])
    for a in (0, 1):
        join(a, 0)
        for at, line in enumerate(lines(flip(places[a], chain - 1), near, chain - 1)):
            for unit in range(near, -1, -1):
                forward(a, chain - 1, (at, unit), *units(line, near)[unit])
    for which in range(1, chain - near + 1):
        for a in (0, 1):
            join(a, which)
    for step in range(chain - 1, near - 1, -1):
        count = 2 ** (step - near)
        for at in range(count):
            for unit in range(near, -1, -1):
                for a in (0, 1):
                    where, size = units(lines(places[a], near, step)[at], near)[unit]
                    copies[a][step, at, unit].wait_recv()
                    accs[a][spot(where, size), :] = add(a, step, where, size).astype(jnp.bfloat16)
                    if step > near and at < count // 2:
                        forward(a, step - 1, (at, unit), where, size)
                    elif step == near and unit == near:
                        forward(a, near - 1, (), where, size)
    for step in range(near - 1, -1, -1):
        for a in (0, 1):
            copies[a][step,].wait_recv()
            if step:
                first = flip(places[a], step - 1)
                accs[a][spot(first, step - 1), :] = add(a, step, first, step - 1).astype(jnp.bfloat16)
                forward(a, step - 1, (), first, step - 1)
                accs[a][spot(places[a], step - 1), :] = add(a, step, places[a], step - 1).astype(jnp.bfloat16)
            else:
                outs[a][...] = add(a, 0, places[a], 0).astype(jnp.bfloat16)
    for a in (0, 1):
        for copy in copies[a].values():
            copy.wait_send()


def attend_kernel(inner, blk_spans, slots, tab_k, tab_v, q_in, do_in, k_ref, v_ref,
                  dq_ref, dk_ref, dv_ref, at_k, at_v, ks, vs, q_ref, do_ref, sem, *kept):
    fetches = [pltpu.make_async_copy(q_in, q_ref, sem.at[0]), pltpu.make_async_copy(do_in, do_ref, sem.at[1])]
    for fetch in fetches:
        fetch.start()
    spans = slots.shape[0]
    span = q_ref.shape[0] // 2
    hd = k_ref.shape[1]
    group = q_ref.shape[1] // hd
    blk = blk_spans * span
    scale = 1.0 / math.sqrt(hd)
    f32 = jnp.float32
    linear = lax.axis_index("outer") * inner + lax.axis_index("inner")

    def note(j, _):
        s = slots[j]
        at_k[s] = tab_k[j] * span
        at_v[s] = tab_v[j] * span
        return 0

    lax.fori_loop(0, spans, note, 0)
    tops = [slots[2 * linear], slots[2 * linear + 1]]
    lasts = [top // blk_spans for top in tops]

    def rows_at(table, s):
        return pl.ds(pl.multiple_of(table[s], span), span)

    nt = (((1,), (1,)), ((), ()))
    tn = (((0,), (0,)), ((), ()))
    width = group * span

    def stack(ref):
        return jnp.concatenate(
            [ref[g * span:(g + 1) * span, h * hd:(h + 1) * hd] for g in (0, 1) for h in range(group)], axis=0)

    for fetch in fetches:
        fetch.wait()
    q, do = stack(q_ref), stack(do_ref)
    lane = lax.broadcasted_iota(jnp.int32, (1, 2 * width), 1)
    q_pos = lane % span + jnp.where(lane < width, tops[0], tops[1]) * span
    low = lax.broadcasted_iota(jnp.int32, (blk, 1), 0)

    def logits(k, n, first, masked):
        t = lax.dot_general(k, q[first:], nt, preferred_element_type=f32) * (scale * LOG2E)
        if masked:
            t = jnp.where(low + n * blk <= q_pos[:, first:], t, NEG_FILL)
        return t

    def stats(n, carry, first, masked):
        top, total, weighted = carry
        at = pl.ds(pl.multiple_of(n * blk, blk), blk)
        spots = [(n * blk_spans + j) for j in range(blk_spans)]
        k = jnp.concatenate([k_ref[rows_at(at_k, s), :] for s in spots], axis=0)
        v = jnp.concatenate([v_ref[rows_at(at_v, s), :] for s in spots], axis=0)
        ks[at, :] = k
        vs[at, :] = v
        t = logits(k, n, first, masked)
        dp = lax.dot_general(v, do[first:], nt, preferred_element_type=f32)
        new = jnp.maximum(top, jnp.max(t, axis=0, keepdims=True))
        shrink = jnp.exp2(top - new)
        e = jnp.exp2(t - new)
        if kept:
            kept[0][at, first:] = e
            kept[1][at, first:] = dp
            kept[2][n, :, first:] = new
        return (new, total * shrink + jnp.sum(e, axis=0, keepdims=True),
                weighted * shrink + jnp.sum(e * dp, axis=0, keepdims=True))

    def sweep(step, carry, narrow):
        carry = lax.fori_loop(0, lasts[0], functools.partial(step, first=0, masked=False), carry)
        carry = step(lasts[0], carry, 0, True)
        late = narrow(carry)
        late = lax.fori_loop(lasts[0] + 1, lasts[1], functools.partial(step, first=width, masked=False), late)
        return carry, step(lasts[1], late, width, True)

    start = (jnp.full((1, 2 * width), NEG_FILL, f32), jnp.zeros((1, 2 * width), f32), jnp.zeros((1, 2 * width), f32))
    early, late = sweep(stats, start, lambda carry: tuple(x[:, width:] for x in carry))
    top, total, weighted = [jnp.concatenate([x[:, :width], y], axis=1) for x, y in zip(early, late)]
    lse = top + jnp.log2(total)
    delta = weighted / total

    def grads(n, dq, first, masked):
        at = pl.ds(pl.multiple_of(n * blk, blk), blk)
        k, v = ks[at, :], vs[at, :]
        if kept:
            p = kept[0][at, first:] * jnp.exp2(kept[2][n, :, first:] - lse[:, first:])
            dp = kept[1][at, first:]
        else:
            p = jnp.exp2(logits(k, n, first, masked) - lse[:, first:])
            dp = lax.dot_general(v, do[first:], nt, preferred_element_type=f32)
        ds = (p * (dp - delta[:, first:]) * scale).astype(jnp.bfloat16)
        dk = jnp.dot(ds, q[first:], preferred_element_type=f32).astype(jnp.bfloat16)
        dv = jnp.dot(p.astype(jnp.bfloat16), do[first:], preferred_element_type=f32).astype(jnp.bfloat16)
        for j in range(blk_spans):
            s = n * blk_spans + j
            dk_ref[rows_at(at_k, s), :] = dk[j * span:(j + 1) * span]
            dv_ref[rows_at(at_v, s), :] = dv[j * span:(j + 1) * span]
        return dq + lax.dot_general(k, ds, tn, preferred_element_type=f32)

    early, late = sweep(grads, jnp.zeros((hd, 2 * width), f32), lambda dq: dq[:, width:])
    dq = jnp.concatenate([early[:, :width], late], axis=1).T
    for g in (0, 1):
        for h in range(group):
            at = (g * group + h) * span
            dq_ref[g * span:(g + 1) * span, h * hd:(h + 1) * hd] = dq[at:at + span].astype(jnp.bfloat16)

    def blank(s, _):
        none = jnp.zeros((span, hd), jnp.bfloat16)
        dk_ref[rows_at(at_k, s), :] = none
        dv_ref[rows_at(at_v, s), :] = none
        return 0

    lax.fori_loop((lasts[1] + 1) * blk_spans, spans, blank, 0)


def local(outer, inner, queries, keys, values, grad_out, span_slot):
    rows, hd = keys.shape
    total = rows * outer * inner
    spans = span_slot.shape[0]
    orders = bits_of(outer, inner)
    low = jnp.bfloat16
    vmem, smem = pl.BlockSpec(memory_space=pltpu.VMEM), pl.BlockSpec(memory_space=pltpu.SMEM)
    moves = moves_of(inner.bit_length() - 1, outer.bit_length() - 2)
    hbm = pl.BlockSpec(memory_space=pltpu.HBM)
    sems = [pltpu.SemaphoreType.DMA((2, moves)), pltpu.SemaphoreType.DMA((2, moves))]
    unit = total * hd
    whole = jax.ShapeDtypeStruct((total, hd), low)
    block = jax.ShapeDtypeStruct((rows, hd), low)
    keys_all, values_all = pl.pallas_call(
        functools.partial(gather_kernel, orders),
        out_shape=(whole, whole), in_specs=[hbm] * 2, out_specs=(vmem, vmem),
        scratch_shapes=sems + [pltpu.SemaphoreType.DMA((2,))],
        compiler_params=pltpu.CompilerParams(
            collective_id=0, has_side_effects=True, vmem_limit_bytes=4 * unit + 4 * MIB),
    )(keys, values)
    tables = [
        jnp.asarray(np.array([2 * place_of(order, j // 2 // inner, j // 2 % inner) + j % 2 for j in range(spans)], np.int32))
        for order in orders
    ]
    blk_spans = math.gcd(spans, 4)
    lanes = rows * queries.shape[1] // hd
    kept = []
    if 8 * total * lanes <= 32 * MIB:
        kept = [pltpu.VMEM((total, lanes), jnp.float32), pltpu.VMEM((total, lanes), jnp.float32),
                pltpu.VMEM((spans // blk_spans, 1, lanes), jnp.float32)]
    grad_queries, dk, dv = pl.pallas_call(
        functools.partial(attend_kernel, inner, blk_spans),
        out_shape=(jax.ShapeDtypeStruct(queries.shape, low), whole, whole),
        in_specs=[smem] * 3 + [hbm] * 2 + [vmem] * 2, out_specs=(vmem, vmem, vmem),
        scratch_shapes=[pltpu.SMEM((spans,), jnp.int32), pltpu.SMEM((spans,), jnp.int32),
                        pltpu.VMEM((total, hd), low), pltpu.VMEM((total, hd), low),
                        pltpu.VMEM(queries.shape, low), pltpu.VMEM(queries.shape, low),
                        pltpu.SemaphoreType.DMA((2,))] + kept,
        compiler_params=pltpu.CompilerParams(
            vmem_limit_bytes=12 * unit + 12 * MIB + (9 * total * lanes if kept else 0)),
    )(span_slot, *tables, queries, grad_out, keys_all, values_all)
    grad_keys, grad_values = pl.pallas_call(
        functools.partial(scatter_kernel, orders),
        out_shape=(block, block), in_specs=[vmem] * 2, out_specs=(vmem, vmem),
        scratch_shapes=[pltpu.VMEM((total // 2, hd), low), pltpu.VMEM((total // 2, hd), low),
                        pltpu.VMEM((total // 2, hd), low), pltpu.VMEM((total // 2, hd), low),
                        pltpu.VMEM((total // 2, hd), low), pltpu.VMEM((total // 2, hd), low)] + sems,
        compiler_params=pltpu.CompilerParams(
            collective_id=1, has_side_effects=True, vmem_limit_bytes=10 * unit + 4 * MIB),
    )(dk, dv)
    return grad_queries, grad_keys, grad_values


def solution(mesh):
    rows = P(("outer", "inner"), None)
    return jax.shard_map(
        functools.partial(local, mesh.shape["outer"], mesh.shape["inner"]),
        mesh=mesh,
        in_specs=(rows, rows, rows, rows, P()),
        out_specs=(rows, rows, rows),
        check_vma=False,
    )
```

```python
import functools
import math

import jax
import jax.numpy as jnp
import numpy as np
from jax import lax
from jax.experimental import pallas as pl
from jax.experimental.pallas import tpu as pltpu
from jax.sharding import PartitionSpec as P

NEG_FILL = -1e30
LOG2E = math.log2(math.e)
MIB = 1024 * 1024
MESH = pl.DeviceIdType.MESH


def bits_of(outer, inner):
    near = [("inner", b) for b in range(inner.bit_length() - 1)]
    chips = [("outer", b) for b in range(1, outer.bit_length() - 1)]
    core = [("outer", 0)]
    return near + chips + core, near[::-1] + chips[::-1] + core


def place_of(order, o, i):
    place = 0
    for at, (axis, b) in enumerate(order):
        place = place + (((o if axis == "outer" else i) // 2**b) % 2) * 2**at
    return place


def partner_of(axis, b, o, i):
    if axis == "outer":
        return (o + (1 - 2 * ((o // 2**b) % 2)) * 2**b, i)
    return (o, i + (1 - 2 * ((i // 2**b) % 2)) * 2**b)


def greet(order, o, i):
    barrier = pltpu.get_barrier_semaphore()
    for axis, b in order:
        pl.semaphore_signal(barrier, inc=1, device_id=partner_of(axis, b, o, i), device_id_type=MESH)
    pl.semaphore_wait(barrier, len(order))


def flip(place, step):
    return place + (1 - 2 * ((place // 2**step) % 2)) * 2**step


def units(place, near):
    return [(place, 0)] + [(flip(place, step), step) for step in range(near)]


def lines(place, near, step):
    if step == near:
        return [place]
    return lines(flip(place, step - 1), near, step - 1) + lines(place, near, step - 1)


def moves_of(near, chips):
    return near + (near + 1) * (2**chips - 1 + 2 ** (chips - 1)) + chips + 2 ** (chips - 1)


def gather_kernel(orders, k_in, v_in, k_out, v_out, send, recv, own):
    o, i = lax.axis_index("outer"), lax.axis_index("inner")
    rows = k_in.shape[0]
    chain = len(orders[0]) - 1
    near = sum(axis == "inner" for axis, _ in orders[0])
    places = [place_of(order, o, i) for order in orders]
    outs = (k_out, v_out)

    def span_of(place, step):
        size = rows * 2**step
        return pl.ds(pl.multiple_of((place // 2**step) * size, size), size)

    owned = [
        pltpu.make_async_copy((k_in, v_in)[a], outs[a].at[span_of(places[a], 0), :], own.at[a]) for a in (0, 1)
    ]
    for copy in owned:
        copy.start()
    greet(orders[0], o, i)
    copies, waited = ({}, {}), set()

    def begin(a, name, part, bit):
        part = outs[a].at[part, :]
        at = len(copies[a])
        copies[a][name] = pltpu.make_async_remote_copy(
            src_ref=part, dst_ref=part, send_sem=send.at[a, at], recv_sem=recv.at[a, at],
            device_id=partner_of(*bit, o, i), device_id_type=MESH)
        copies[a][name].start()

    def arrive(a, name):
        copies[a][name].wait_recv()
        waited.add((a, name))

    def spread(a, path, unit, step):
        place = places[a]
        for bit in path:
            place = flip(place, bit)
        where, size = units(place, near)[unit]
        for later in range(step, chain):
            begin(a, (path + (later,), unit), span_of(where, size), orders[a][later])

    paths = [()]
    for bit in range(near, chain):
        paths = paths + [path + (bit,) for path in paths]
    for a in (0, 1):
        owned[a].wait()
        begin(a, 0, span_of(places[a], 0), orders[a][0])
    for a in (0, 1):
        spread(a, (), 0, near)
    for unit in range(near + 1):
        if unit:
            for a in (0, 1):
                arrive(a, unit - 1)
                if unit < near:
                    begin(a, unit, span_of(places[a], unit), orders[a][unit])
                spread(a, (), unit, near)
                if unit == near:
                    begin(a, "core", span_of(places[a], near), orders[a][chain])
        for path in paths[1:]:
            if path[-1] < chain - 1:
                for a in (0, 1):
                    arrive(a, (path, unit))
                    spread(a, path, unit, path[-1] + 1)
    for bit in range(near, chain - 1):
        for a in (0, 1):
            begin(a, ("core", bit), span_of(flip(places[a], bit), bit), orders[a][chain])
    for unit in range(near + 1):
        for path in paths[1:]:
            if path[-1] == chain - 1:
                for a in (0, 1):
                    arrive(a, (path, unit))
                    place = places[a]
                    for bit in path:
                        place = flip(place, bit)
                    where, size = units(place, near)[unit]
                    begin(a, ("core", path, unit), span_of(where, size), orders[a][chain])
    for a in (0, 1):
        for name, copy in copies[a].items():
            copy.wait_send()
            if (a, name) not in waited:
                copy.wait_recv()


def scatter_kernel(orders, k_in, v_in, k_out, v_out, k_acc, v_acc, k_got, v_got, k_core, v_core, send, recv):
    o, i = lax.axis_index("outer"), lax.axis_index("inner")
    rows = k_out.shape[0]
    chain = len(orders[0]) - 1
    near = sum(axis == "inner" for axis, _ in orders[0])
    greet(orders[0], o, i)
    half = 2**chain
    ins, outs, accs = (k_in, v_in), (k_out, v_out), (k_acc, v_acc)
    gots, cores = (k_got, v_got), (k_core, v_core)
    full = [place_of(order, o, i) for order in orders]
    places = [place % half for place in full]
    sides = [place // half for place in full]
    copies = ({}, {})

    def spot(place, step, offset=0):
        size = rows * 2**step
        return pl.ds(pl.multiple_of((place // 2**step) * size + offset, size), size)

    def begin(a, name, src, dst, bit):
        at = len(copies[a])
        copies[a][name] = pltpu.make_async_remote_copy(
            src_ref=src, dst_ref=dst, send_sem=send.at[a, at], recv_sem=recv.at[a, at],
            device_id=partner_of(*bit, o, i), device_id_type=MESH)
        copies[a][name].start()

    def landing(step, place, size):
        return spot(place % 2**step, size, rows * 2**step)

    def forward(a, step, name, place, size):
        begin(a, (step,) + name, accs[a].at[spot(place, size), :], gots[a].at[landing(step, place, size), :],
              orders[a][step])

    def add(a, step, place, size):
        got = gots[a][landing(step, place, size), :]
        return accs[a][spot(place, size), :].astype(jnp.float32) + got.astype(jnp.float32)

    def pieces(a):
        return [(line, near) for line in lines(flip(places[a], chain - 1), near, chain - 1)] + [
            (flip(places[a], step), step) for step in range(chain - 2, near - 1, -1)] + [(places[a], near)]

    def join(a, which):
        place, step = pieces(a)[which]
        copies[a]["core", which].wait_recv()
        mine = ins[a][spot(place, step, sides[a] * half * rows), :]
        total = mine.astype(jnp.float32) + cores[a][spot(place, step), :].astype(jnp.float32)
        accs[a][spot(place, step), :] = total.astype(jnp.bfloat16)

    ahead = 2 ** (chain - 1 - near)
    for which in range(ahead + chain - near):
        for a in (0, 1):
            place, step = pieces(a)[which]
            begin(a, ("core", which), ins[a].at[spot(place, step, (1 - sides[a]) * half * rows), :],
                  cores[a].at[spot(place, step), :], orders[a][chain])
    for at in range(ahead):
        for a in (0, 1):
            join(a, at)
            for unit in range(near, -1, -1):
                forward(a, chain - 1, (at, unit), *units(pieces(a)[at][0], near)[unit])
    for which in range(ahead, ahead + chain - near):
        for a in (0, 1):
            join(a, which)
    for step in range(chain - 1, near - 1, -1):
        count = 2 ** (step - near)
        for at in range(count):
            for unit in range(near, -1, -1):
                for a in (0, 1):
                    where, size = units(lines(places[a], near, step)[at], near)[unit]
                    copies[a][step, at, unit].wait_recv()
                    accs[a][spot(where, size), :] = add(a, step, where, size).astype(jnp.bfloat16)
                    if step > near and at < count // 2:
                        forward(a, step - 1, (at, unit), where, size)
                    elif step == near and unit == near:
                        forward(a, near - 1, (), where, size)
    for step in range(near - 1, -1, -1):
        for a in (0, 1):
            copies[a][step,].wait_recv()
            if step:
                first = flip(places[a], step - 1)
                accs[a][spot(first, step - 1), :] = add(a, step, first, step - 1).astype(jnp.bfloat16)
                forward(a, step - 1, (), first, step - 1)
                accs[a][spot(places[a], step - 1), :] = add(a, step, places[a], step - 1).astype(jnp.bfloat16)
            else:
                outs[a][...] = add(a, 0, places[a], 0).astype(jnp.bfloat16)
    for a in (0, 1):
        for copy in copies[a].values():
            copy.wait_send()


def attend_kernel(inner, blk_spans, slots, tab_k, tab_v, q_in, do_in, k_ref, v_ref,
                  dq_ref, dk_ref, dv_ref, at_k, at_v, ks, vs, q_ref, do_ref, sem, *kept):
    fetches = [pltpu.make_async_copy(q_in, q_ref, sem.at[0]), pltpu.make_async_copy(do_in, do_ref, sem.at[1])]
    for fetch in fetches:
        fetch.start()
    spans = slots.shape[0]
    span = q_ref.shape[0] // 2
    hd = k_ref.shape[1]
    group = q_ref.shape[1] // hd
    blk = blk_spans * span
    scale = 1.0 / math.sqrt(hd)
    f32 = jnp.float32
    linear = lax.axis_index("outer") * inner + lax.axis_index("inner")

    def note(j, _):
        s = slots[j]
        at_k[s] = tab_k[j] * span
        at_v[s] = tab_v[j] * span
        return 0

    lax.fori_loop(0, spans, note, 0)
    tops = [slots[2 * linear], slots[2 * linear + 1]]
    lasts = [top // blk_spans for top in tops]

    def rows_at(table, s):
        return pl.ds(pl.multiple_of(table[s], span), span)

    nt = (((1,), (1,)), ((), ()))
    tn = (((0,), (0,)), ((), ()))
    width = group * span

    def stack(ref):
        return jnp.concatenate(
            [ref[g * span:(g + 1) * span, h * hd:(h + 1) * hd] for g in (0, 1) for h in range(group)], axis=0)

    for fetch in fetches:
        fetch.wait()
    q, do = stack(q_ref), stack(do_ref)
    lane = lax.broadcasted_iota(jnp.int32, (1, 2 * width), 1)
    q_pos = lane % span + jnp.where(lane < width, tops[0], tops[1]) * span
    low = lax.broadcasted_iota(jnp.int32, (blk, 1), 0)

    def logits(k, n, first, masked):
        t = lax.dot_general(k, q[first:], nt, preferred_element_type=f32) * (scale * LOG2E)
        if masked:
            t = jnp.where(low + n * blk <= q_pos[:, first:], t, NEG_FILL)
        return t

    def stats(n, carry, first, masked):
        top, total, weighted = carry
        at = pl.ds(pl.multiple_of(n * blk, blk), blk)
        spots = [(n * blk_spans + j) for j in range(blk_spans)]
        k = jnp.concatenate([k_ref[rows_at(at_k, s), :] for s in spots], axis=0)
        v = jnp.concatenate([v_ref[rows_at(at_v, s), :] for s in spots], axis=0)
        ks[at, :] = k
        vs[at, :] = v
        t = logits(k, n, first, masked)
        dp = lax.dot_general(v, do[first:], nt, preferred_element_type=f32)
        new = jnp.maximum(top, jnp.max(t, axis=0, keepdims=True))
        shrink = jnp.exp2(top - new)
        e = jnp.exp2(t - new)
        if kept:
            kept[0][at, first:] = e
            kept[1][at, first:] = dp
            kept[2][n, :, first:] = new
        return (new, total * shrink + jnp.sum(e, axis=0, keepdims=True),
                weighted * shrink + jnp.sum(e * dp, axis=0, keepdims=True))

    def sweep(step, carry, narrow):
        carry = lax.fori_loop(0, lasts[0], functools.partial(step, first=0, masked=False), carry)
        carry = step(lasts[0], carry, 0, True)
        late = narrow(carry)
        late = lax.fori_loop(lasts[0] + 1, lasts[1], functools.partial(step, first=width, masked=False), late)
        return carry, step(lasts[1], late, width, True)

    start = (jnp.full((1, 2 * width), NEG_FILL, f32), jnp.zeros((1, 2 * width), f32), jnp.zeros((1, 2 * width), f32))
    early, late = sweep(stats, start, lambda carry: tuple(x[:, width:] for x in carry))
    top, total, weighted = [jnp.concatenate([x[:, :width], y], axis=1) for x, y in zip(early, late)]
    lse = top + jnp.log2(total)
    delta = weighted / total

    def grads(n, dq, first, masked):
        at = pl.ds(pl.multiple_of(n * blk, blk), blk)
        k, v = ks[at, :], vs[at, :]
        if kept:
            p = kept[0][at, first:] * jnp.exp2(kept[2][n, :, first:] - lse[:, first:])
            dp = kept[1][at, first:]
        else:
            p = jnp.exp2(logits(k, n, first, masked) - lse[:, first:])
            dp = lax.dot_general(v, do[first:], nt, preferred_element_type=f32)
        ds = (p * (dp - delta[:, first:]) * scale).astype(jnp.bfloat16)
        dk = jnp.dot(ds, q[first:], preferred_element_type=f32).astype(jnp.bfloat16)
        dv = jnp.dot(p.astype(jnp.bfloat16), do[first:], preferred_element_type=f32).astype(jnp.bfloat16)
        for j in range(blk_spans):
            s = n * blk_spans + j
            dk_ref[rows_at(at_k, s), :] = dk[j * span:(j + 1) * span]
            dv_ref[rows_at(at_v, s), :] = dv[j * span:(j + 1) * span]
        return dq + lax.dot_general(k, ds, tn, preferred_element_type=f32)

    early, late = sweep(grads, jnp.zeros((hd, 2 * width), f32), lambda dq: dq[:, width:])
    dq = jnp.concatenate([early[:, :width], late], axis=1).T
    for g in (0, 1):
        for h in range(group):
            at = (g * group + h) * span
            dq_ref[g * span:(g + 1) * span, h * hd:(h + 1) * hd] = dq[at:at + span].astype(jnp.bfloat16)

    def blank(s, _):
        none = jnp.zeros((span, hd), jnp.bfloat16)
        dk_ref[rows_at(at_k, s), :] = none
        dv_ref[rows_at(at_v, s), :] = none
        return 0

    lax.fori_loop((lasts[1] + 1) * blk_spans, spans, blank, 0)


def local(outer, inner, queries, keys, values, grad_out, span_slot):
    rows, hd = keys.shape
    total = rows * outer * inner
    spans = span_slot.shape[0]
    orders = bits_of(outer, inner)
    low = jnp.bfloat16
    vmem, smem = pl.BlockSpec(memory_space=pltpu.VMEM), pl.BlockSpec(memory_space=pltpu.SMEM)
    moves = moves_of(inner.bit_length() - 1, outer.bit_length() - 2)
    hbm = pl.BlockSpec(memory_space=pltpu.HBM)
    sems = [pltpu.SemaphoreType.DMA((2, moves)), pltpu.SemaphoreType.DMA((2, moves))]
    unit = total * hd
    whole = jax.ShapeDtypeStruct((total, hd), low)
    block = jax.ShapeDtypeStruct((rows, hd), low)
    keys_all, values_all = pl.pallas_call(
        functools.partial(gather_kernel, orders),
        out_shape=(whole, whole), in_specs=[hbm] * 2, out_specs=(vmem, vmem),
        scratch_shapes=sems + [pltpu.SemaphoreType.DMA((2,))],
        compiler_params=pltpu.CompilerParams(
            collective_id=0, has_side_effects=True, vmem_limit_bytes=4 * unit + 4 * MIB),
    )(keys, values)
    tables = [
        jnp.asarray(np.array([2 * place_of(order, j // 2 // inner, j // 2 % inner) + j % 2 for j in range(spans)], np.int32))
        for order in orders
    ]
    blk_spans = math.gcd(spans, 4)
    lanes = rows * queries.shape[1] // hd
    kept = []
    if 8 * total * lanes <= 32 * MIB:
        kept = [pltpu.VMEM((total, lanes), jnp.float32), pltpu.VMEM((total, lanes), jnp.float32),
                pltpu.VMEM((spans // blk_spans, 1, lanes), jnp.float32)]
    grad_queries, dk, dv = pl.pallas_call(
        functools.partial(attend_kernel, inner, blk_spans),
        out_shape=(jax.ShapeDtypeStruct(queries.shape, low), whole, whole),
        in_specs=[smem] * 3 + [hbm] * 2 + [vmem] * 2, out_specs=(vmem, vmem, vmem),
        scratch_shapes=[pltpu.SMEM((spans,), jnp.int32), pltpu.SMEM((spans,), jnp.int32),
                        pltpu.VMEM((total, hd), low), pltpu.VMEM((total, hd), low),
                        pltpu.VMEM(queries.shape, low), pltpu.VMEM(queries.shape, low),
                        pltpu.SemaphoreType.DMA((2,))] + kept,
        compiler_params=pltpu.CompilerParams(
            vmem_limit_bytes=12 * unit + 12 * MIB + (9 * total * lanes if kept else 0)),
    )(span_slot, *tables, queries, grad_out, keys_all, values_all)
    grad_keys, grad_values = pl.pallas_call(
        functools.partial(scatter_kernel, orders),
        out_shape=(block, block), in_specs=[vmem] * 2, out_specs=(vmem, vmem),
        scratch_shapes=[pltpu.VMEM((total // 2, hd), low), pltpu.VMEM((total // 2, hd), low),
                        pltpu.VMEM((total // 2, hd), low), pltpu.VMEM((total // 2, hd), low),
                        pltpu.VMEM((total // 2, hd), low), pltpu.VMEM((total // 2, hd), low)] + sems,
        compiler_params=pltpu.CompilerParams(
            collective_id=1, has_side_effects=True, vmem_limit_bytes=10 * unit + 4 * MIB),
    )(dk, dv)
    return grad_queries, grad_keys, grad_values


def solution(mesh):
    rows = P(("outer", "inner"), None)
    return jax.shard_map(
        functools.partial(local, mesh.shape["outer"], mesh.shape["inner"]),
        mesh=mesh,
        in_specs=(rows, rows, rows, rows, P()),
        out_specs=(rows, rows, rows),
        check_vma=False,
    )
```

```python
import functools
import math

import jax
import jax.numpy as jnp
import numpy as np
from jax import lax
from jax.experimental import pallas as pl
from jax.experimental.pallas import tpu as pltpu
from jax.sharding import PartitionSpec as P

NEG_FILL = -1e30
LOG2E = math.log2(math.e)
MIB = 1024 * 1024
MESH = pl.DeviceIdType.MESH


def bits_of(outer, inner):
    near = [("inner", b) for b in range(inner.bit_length() - 1)]
    chips = [("outer", b) for b in range(1, outer.bit_length() - 1)]
    core = [("outer", 0)]
    return near + chips + core, near[::-1] + chips[::-1] + core


def place_of(order, o, i):
    place = 0
    for at, (axis, b) in enumerate(order):
        place = place + (((o if axis == "outer" else i) // 2**b) % 2) * 2**at
    return place


def partner_of(axis, b, o, i):
    if axis == "outer":
        return (o + (1 - 2 * ((o // 2**b) % 2)) * 2**b, i)
    return (o, i + (1 - 2 * ((i // 2**b) % 2)) * 2**b)


def greet(order, o, i):
    barrier = pltpu.get_barrier_semaphore()
    for axis, b in order:
        pl.semaphore_signal(barrier, inc=1, device_id=partner_of(axis, b, o, i), device_id_type=MESH)
    pl.semaphore_wait(barrier, len(order))


def flip(place, step):
    return place + (1 - 2 * ((place // 2**step) % 2)) * 2**step


def units(place, near):
    return [(place, 0)] + [(flip(place, step), step) for step in range(near)]


def lines(place, near, step):
    if step == near:
        return [place]
    return lines(flip(place, step - 1), near, step - 1) + lines(place, near, step - 1)


def moves_of(near, chips):
    return near + (near + 1) * (2**chips - 1 + 2 ** (chips - 1)) + chips + 2 ** (chips - 1)


def gather_kernel(orders, k_in, v_in, k_out, v_out, send, recv, own):
    o, i = lax.axis_index("outer"), lax.axis_index("inner")
    rows = k_in.shape[0]
    chain = len(orders[0]) - 1
    near = sum(axis == "inner" for axis, _ in orders[0])
    places = [place_of(order, o, i) for order in orders]
    outs = (k_out, v_out)

    def span_of(place, step):
        size = rows * 2**step
        return pl.ds(pl.multiple_of((place // 2**step) * size, size), size)

    owned = [
        pltpu.make_async_copy((k_in, v_in)[a], outs[a].at[span_of(places[a], 0), :], own.at[a]) for a in (0, 1)
    ]
    for copy in owned:
        copy.start()
    greet(orders[0], o, i)
    copies, waited = ({}, {}), set()

    def begin(a, name, part, bit):
        part = outs[a].at[part, :]
        at = len(copies[a])
        copies[a][name] = pltpu.make_async_remote_copy(
            src_ref=part, dst_ref=part, send_sem=send.at[a, at], recv_sem=recv.at[a, at],
            device_id=partner_of(*bit, o, i), device_id_type=MESH)
        copies[a][name].start()

    def arrive(a, name):
        copies[a][name].wait_recv()
        waited.add((a, name))

    def spread(a, path, unit, step):
        place = places[a]
        for bit in path:
            place = flip(place, bit)
        where, size = units(place, near)[unit]
        for later in range(step, chain):
            begin(a, (path + (later,), unit), span_of(where, size), orders[a][later])

    paths = [()]
    for bit in range(near, chain):
        paths = paths + [path + (bit,) for path in paths]
    for a in (0, 1):
        owned[a].wait()
        begin(a, 0, span_of(places[a], 0), orders[a][0])
    for a in (0, 1):
        spread(a, (), 0, near)
    for unit in range(near + 1):
        if unit:
            for a in (0, 1):
                arrive(a, unit - 1)
                if unit < near:
                    begin(a, unit, span_of(places[a], unit), orders[a][unit])
                spread(a, (), unit, near)
                if unit == near:
                    begin(a, "core", span_of(places[a], near), orders[a][chain])
        for path in paths[1:]:
            if path[-1] < chain - 1:
                for a in (0, 1):
                    arrive(a, (path, unit))
                    spread(a, path, unit, path[-1] + 1)
    for bit in range(near, chain - 1):
        for a in (0, 1):
            begin(a, ("core", bit), span_of(flip(places[a], bit), bit), orders[a][chain])
    for unit in range(near + 1):
        for path in paths[1:]:
            if path[-1] == chain - 1:
                for a in (0, 1):
                    arrive(a, (path, unit))
                    place = places[a]
                    for bit in path:
                        place = flip(place, bit)
                    where, size = units(place, near)[unit]
                    begin(a, ("core", path, unit), span_of(where, size), orders[a][chain])
    for a in (0, 1):
        for name, copy in copies[a].items():
            copy.wait_send()
            if (a, name) not in waited:
                copy.wait_recv()


def scatter_kernel(orders, k_in, v_in, k_out, v_out, k_acc, v_acc, k_got, v_got, k_core, v_core, send, recv):
    o, i = lax.axis_index("outer"), lax.axis_index("inner")
    rows = k_out.shape[0]
    chain = len(orders[0]) - 1
    near = sum(axis == "inner" for axis, _ in orders[0])
    greet(orders[0], o, i)
    half = 2**chain
    ins, outs, accs = (k_in, v_in), (k_out, v_out), (k_acc, v_acc)
    gots, cores = (k_got, v_got), (k_core, v_core)
    full = [place_of(order, o, i) for order in orders]
    places = [place % half for place in full]
    sides = [place // half for place in full]
    copies = ({}, {})

    def spot(place, step, offset=0):
        size = rows * 2**step
        return pl.ds(pl.multiple_of((place // 2**step) * size + offset, size), size)

    def begin(a, name, src, dst, bit):
        at = len(copies[a])
        copies[a][name] = pltpu.make_async_remote_copy(
            src_ref=src, dst_ref=dst, send_sem=send.at[a, at], recv_sem=recv.at[a, at],
            device_id=partner_of(*bit, o, i), device_id_type=MESH)
        copies[a][name].start()

    def landing(step, place, size):
        return spot(place % 2**step, size, rows * 2**step)

    def forward(a, step, name, place, size):
        begin(a, (step,) + name, accs[a].at[spot(place, size), :], gots[a].at[landing(step, place, size), :],
              orders[a][step])

    def add(a, step, place, size):
        got = gots[a][landing(step, place, size), :]
        return accs[a][spot(place, size), :].astype(jnp.float32) + got.astype(jnp.float32)

    def pieces(a):
        return [(line, near) for line in lines(flip(places[a], chain - 1), near, chain - 1)] + [
            (flip(places[a], step), step) for step in range(chain - 2, near - 1, -1)] + [(places[a], near)]

    def join(a, which):
        place, step = pieces(a)[which]
        copies[a]["core", which].wait_recv()
        mine = ins[a][spot(place, step, sides[a] * half * rows), :]
        total = mine.astype(jnp.float32) + cores[a][spot(place, step), :].astype(jnp.float32)
        accs[a][spot(place, step), :] = total.astype(jnp.bfloat16)

    ahead = 2 ** (chain - 1 - near)
    for which in range(ahead + chain - near):
        for a in (0, 1):
            place, step = pieces(a)[which]
            begin(a, ("core", which), ins[a].at[spot(place, step, (1 - sides[a]) * half * rows), :],
                  cores[a].at[spot(place, step), :], orders[a][chain])
    for at in range(ahead):
        for a in (0, 1):
            join(a, at)
            for unit in range(near, -1, -1):
                forward(a, chain - 1, (at, unit), *units(pieces(a)[at][0], near)[unit])
    for which in range(ahead, ahead + chain - near):
        for a in (0, 1):
            join(a, which)
    for step in range(chain - 1, near - 1, -1):
        count = 2 ** (step - near)
        for at in range(count):
            for unit in range(near, -1, -1):
                for a in (0, 1):
                    where, size = units(lines(places[a], near, step)[at], near)[unit]
                    copies[a][step, at, unit].wait_recv()
                    accs[a][spot(where, size), :] = add(a, step, where, size).astype(jnp.bfloat16)
                    if step > near and at < count // 2:
                        forward(a, step - 1, (at, unit), where, size)
                    elif step == near and unit == near:
                        forward(a, near - 1, (), where, size)
    for step in range(near - 1, -1, -1):
        for a in (0, 1):
            copies[a][step,].wait_recv()
            if step:
                first = flip(places[a], step - 1)
                accs[a][spot(first, step - 1), :] = add(a, step, first, step - 1).astype(jnp.bfloat16)
                forward(a, step - 1, (), first, step - 1)
                accs[a][spot(places[a], step - 1), :] = add(a, step, places[a], step - 1).astype(jnp.bfloat16)
            else:
                outs[a][...] = add(a, 0, places[a], 0).astype(jnp.bfloat16)
    for a in (0, 1):
        for copy in copies[a].values():
            copy.wait_send()


def attend_kernel(inner, blk_spans, slots, tab_k, tab_v, q_ref, do_ref, k_ref, v_ref,
                  dq_ref, dk_ref, dv_ref, at_k, at_v, ks, vs, *kept):
    spans = slots.shape[0]
    span = q_ref.shape[0] // 2
    hd = k_ref.shape[1]
    group = q_ref.shape[1] // hd
    blk = blk_spans * span
    scale = 1.0 / math.sqrt(hd)
    f32 = jnp.float32
    linear = lax.axis_index("outer") * inner + lax.axis_index("inner")

    def note(j, _):
        s = slots[j]
        at_k[s] = tab_k[j] * span
        at_v[s] = tab_v[j] * span
        return 0

    lax.fori_loop(0, spans, note, 0)
    tops = [slots[2 * linear], slots[2 * linear + 1]]
    lasts = [top // blk_spans for top in tops]

    def rows_at(table, s):
        return pl.ds(pl.multiple_of(table[s], span), span)

    nt = (((1,), (1,)), ((), ()))
    tn = (((0,), (0,)), ((), ()))
    width = group * span

    def stack(ref):
        return jnp.concatenate(
            [ref[g * span:(g + 1) * span, h * hd:(h + 1) * hd] for g in (0, 1) for h in range(group)], axis=0)

    q, do = stack(q_ref), stack(do_ref)
    lane = lax.broadcasted_iota(jnp.int32, (1, 2 * width), 1)
    q_pos = lane % span + jnp.where(lane < width, tops[0], tops[1]) * span
    low = lax.broadcasted_iota(jnp.int32, (blk, 1), 0)

    def logits(k, n, first, masked):
        t = lax.dot_general(k, q[first:], nt, preferred_element_type=f32) * (scale * LOG2E)
        if masked:
            t = jnp.where(low + n * blk <= q_pos[:, first:], t, NEG_FILL)
        return t

    def stats(n, carry, first, masked, blocks=1):
        top, total, weighted = carry
        at = pl.ds(pl.multiple_of(n * blk, blk), blocks * blk)
        spots = [(n * blk_spans + j) for j in range(blocks * blk_spans)]
        k = jnp.concatenate([k_ref[rows_at(at_k, s), :] for s in spots], axis=0)
        v = jnp.concatenate([v_ref[rows_at(at_v, s), :] for s in spots], axis=0)
        ks[at, :] = k
        vs[at, :] = v
        t = logits(k, n, first, masked)
        dp = lax.dot_general(v, do[first:], nt, preferred_element_type=f32)
        new = jnp.maximum(top, jnp.max(t, axis=0, keepdims=True))
        shrink = jnp.exp2(top - new)
        e = jnp.exp2(t - new)
        if kept:
            kept[0][at, first:] = e
            kept[1][at, first:] = dp
            kept[2][n, :, first:] = new
        return (new, total * shrink + jnp.sum(e, axis=0, keepdims=True),
                weighted * shrink + jnp.sum(e * dp, axis=0, keepdims=True))

    def run(step, begin, end, first, carry):
        pairs = (end - begin) // 2
        carry = lax.fori_loop(
            0, pairs, lambda n, c: step(begin + 2 * n, c, first, False, 2), carry)
        return lax.fori_loop(begin + 2 * pairs, end, lambda n, c: step(n, c, first, False), carry)

    def sweep(step, carry, narrow):
        carry = run(step, 0, lasts[0], 0, carry)
        carry = step(lasts[0], carry, 0, True)
        late = run(step, lasts[0] + 1, lasts[1], width, narrow(carry))
        return carry, step(lasts[1], late, width, True)

    start = (jnp.full((1, 2 * width), NEG_FILL, f32), jnp.zeros((1, 2 * width), f32), jnp.zeros((1, 2 * width), f32))
    early, late = sweep(stats, start, lambda carry: tuple(x[:, width:] for x in carry))
    top, total, weighted = [jnp.concatenate([x[:, :width], y], axis=1) for x, y in zip(early, late)]
    lse = top + jnp.log2(total)
    delta = weighted / total

    def grads(n, dq, first, masked, blocks=1):
        at = pl.ds(pl.multiple_of(n * blk, blk), blocks * blk)
        k, v = ks[at, :], vs[at, :]
        if kept:
            p = kept[0][at, first:] * jnp.exp2(kept[2][n, :, first:] - lse[:, first:])
            dp = kept[1][at, first:]
        else:
            p = jnp.exp2(logits(k, n, first, masked) - lse[:, first:])
            dp = lax.dot_general(v, do[first:], nt, preferred_element_type=f32)
        ds = (p * (dp - delta[:, first:]) * scale).astype(jnp.bfloat16)
        dk = jnp.dot(ds, q[first:], preferred_element_type=f32).astype(jnp.bfloat16)
        dv = jnp.dot(p.astype(jnp.bfloat16), do[first:], preferred_element_type=f32).astype(jnp.bfloat16)
        for j in range(blocks * blk_spans):
            s = n * blk_spans + j
            dk_ref[rows_at(at_k, s), :] = dk[j * span:(j + 1) * span]
            dv_ref[rows_at(at_v, s), :] = dv[j * span:(j + 1) * span]
        return dq + lax.dot_general(k, ds, tn, preferred_element_type=f32)

    early, late = sweep(grads, jnp.zeros((hd, 2 * width), f32), lambda dq: dq[:, width:])
    dq = jnp.concatenate([early[:, :width], late], axis=1).T
    for g in (0, 1):
        for h in range(group):
            at = (g * group + h) * span
            dq_ref[g * span:(g + 1) * span, h * hd:(h + 1) * hd] = dq[at:at + span].astype(jnp.bfloat16)

    def blank(s, _):
        none = jnp.zeros((span, hd), jnp.bfloat16)
        dk_ref[rows_at(at_k, s), :] = none
        dv_ref[rows_at(at_v, s), :] = none
        return 0

    lax.fori_loop((lasts[1] + 1) * blk_spans, spans, blank, 0)


def local(outer, inner, queries, keys, values, grad_out, span_slot):
    rows, hd = keys.shape
    total = rows * outer * inner
    spans = span_slot.shape[0]
    orders = bits_of(outer, inner)
    low = jnp.bfloat16
    vmem, smem = pl.BlockSpec(memory_space=pltpu.VMEM), pl.BlockSpec(memory_space=pltpu.SMEM)
    moves = moves_of(inner.bit_length() - 1, outer.bit_length() - 2)
    hbm = pl.BlockSpec(memory_space=pltpu.HBM)
    sems = [pltpu.SemaphoreType.DMA((2, moves)), pltpu.SemaphoreType.DMA((2, moves))]
    unit = total * hd
    whole = jax.ShapeDtypeStruct((total, hd), low)
    block = jax.ShapeDtypeStruct((rows, hd), low)
    keys_all, values_all = pl.pallas_call(
        functools.partial(gather_kernel, orders),
        out_shape=(whole, whole), in_specs=[hbm] * 2, out_specs=(vmem, vmem),
        scratch_shapes=sems + [pltpu.SemaphoreType.DMA((2,))],
        compiler_params=pltpu.CompilerParams(
            collective_id=0, has_side_effects=True, vmem_limit_bytes=4 * unit + 4 * MIB),
        cost_estimate=pl.CostEstimate(flops=0, bytes_accessed=64 * unit, transcendentals=0),
    )(keys, values)
    tables = [
        jnp.asarray(np.array([2 * place_of(order, j // 2 // inner, j // 2 % inner) + j % 2 for j in range(spans)], np.int32))
        for order in orders
    ]
    blk_spans = math.gcd(spans, 4)
    lanes = rows * queries.shape[1] // hd
    kept = []
    if 8 * total * lanes <= 32 * MIB:
        kept = [pltpu.VMEM((total, lanes), jnp.float32), pltpu.VMEM((total, lanes), jnp.float32),
                pltpu.VMEM((spans // blk_spans, 1, lanes), jnp.float32)]
    grad_queries, dk, dv = pl.pallas_call(
        functools.partial(attend_kernel, inner, blk_spans),
        out_shape=(jax.ShapeDtypeStruct(queries.shape, low), whole, whole),
        in_specs=[smem] * 3 + [vmem] * 4, out_specs=(vmem, vmem, vmem),
        scratch_shapes=[pltpu.SMEM((spans,), jnp.int32), pltpu.SMEM((spans,), jnp.int32),
                        pltpu.VMEM((total, hd), low), pltpu.VMEM((total, hd), low)] + kept,
        compiler_params=pltpu.CompilerParams(
            vmem_limit_bytes=12 * unit + 12 * MIB + (9 * total * lanes if kept else 0)),
    )(span_slot, *tables, queries, grad_out, keys_all, values_all)
    grad_keys, grad_values = pl.pallas_call(
        functools.partial(scatter_kernel, orders),
        out_shape=(block, block), in_specs=[vmem] * 2, out_specs=(vmem, vmem),
        scratch_shapes=[pltpu.VMEM((total // 2, hd), low), pltpu.VMEM((total // 2, hd), low),
                        pltpu.VMEM((total // 2, hd), low), pltpu.VMEM((total // 2, hd), low),
                        pltpu.VMEM((total // 2, hd), low), pltpu.VMEM((total // 2, hd), low)] + sems,
        compiler_params=pltpu.CompilerParams(
            collective_id=1, has_side_effects=True, vmem_limit_bytes=10 * unit + 4 * MIB),
    )(dk, dv)
    return grad_queries, grad_keys, grad_values


def solution(mesh):
    rows = P(("outer", "inner"), None)
    return jax.shard_map(
        functools.partial(local, mesh.shape["outer"], mesh.shape["inner"]),
        mesh=mesh,
        in_specs=(rows, rows, rows, rows, P()),
        out_specs=(rows, rows, rows),
        check_vma=False,
    )
```

```python
import functools
import math

import jax
import jax.numpy as jnp
import numpy as np
from jax import lax
from jax.experimental import pallas as pl
from jax.experimental.pallas import tpu as pltpu
from jax.sharding import PartitionSpec as P

NEG_FILL = -1e30
LOG2E = math.log2(math.e)
MIB = 1024 * 1024
MESH = pl.DeviceIdType.MESH


def bits_of(outer, inner):
    near = [("inner", b) for b in range(inner.bit_length() - 1)]
    chips = [("outer", b) for b in range(1, outer.bit_length() - 1)]
    core = [("outer", 0)]
    return near + chips + core, near[::-1] + chips[::-1] + core


def place_of(order, o, i):
    place = 0
    for at, (axis, b) in enumerate(order):
        place = place + (((o if axis == "outer" else i) // 2**b) % 2) * 2**at
    return place


def partner_of(axis, b, o, i):
    if axis == "outer":
        return (o + (1 - 2 * ((o // 2**b) % 2)) * 2**b, i)
    return (o, i + (1 - 2 * ((i // 2**b) % 2)) * 2**b)


def greet(order, o, i):
    barrier = pltpu.get_barrier_semaphore()
    for axis, b in order:
        pl.semaphore_signal(barrier, inc=1, device_id=partner_of(axis, b, o, i), device_id_type=MESH)
    pl.semaphore_wait(barrier, len(order))


def flip(place, step):
    return place + (1 - 2 * ((place // 2**step) % 2)) * 2**step


def units(place, near):
    return [(place, 0)] + [(flip(place, step), step) for step in range(near)]


def lines(place, near, step):
    if step == near:
        return [place]
    return lines(flip(place, step - 1), near, step - 1) + lines(place, near, step - 1)


def moves_of(near, chips):
    return near + (near + 1) * (2**chips - 1 + 2 ** (chips - 1)) + chips + 2 ** (chips - 1)


def gather_kernel(orders, k_in, v_in, q_in, do_in, k_out, v_out, q_out, do_out, send, recv, own):
    o, i = lax.axis_index("outer"), lax.axis_index("inner")
    rows = k_in.shape[0]
    chain = len(orders[0]) - 1
    near = sum(axis == "inner" for axis, _ in orders[0])
    places = [place_of(order, o, i) for order in orders]
    outs = (k_out, v_out)

    def span_of(place, step):
        size = rows * 2**step
        return pl.ds(pl.multiple_of((place // 2**step) * size, size), size)

    owned = [
        pltpu.make_async_copy((k_in, v_in)[a], outs[a].at[span_of(places[a], 0), :], own.at[a]) for a in (0, 1)
    ]
    fetches = [pltpu.make_async_copy(q_in, q_out, own.at[2]), pltpu.make_async_copy(do_in, do_out, own.at[3])]
    for copy in owned + fetches:
        copy.start()
    greet(orders[0], o, i)
    copies, waited = ({}, {}), set()

    def begin(a, name, part, bit):
        part = outs[a].at[part, :]
        at = len(copies[a])
        copies[a][name] = pltpu.make_async_remote_copy(
            src_ref=part, dst_ref=part, send_sem=send.at[a, at], recv_sem=recv.at[a, at],
            device_id=partner_of(*bit, o, i), device_id_type=MESH)
        copies[a][name].start()

    def arrive(a, name):
        copies[a][name].wait_recv()
        waited.add((a, name))

    def spread(a, path, unit, step):
        place = places[a]
        for bit in path:
            place = flip(place, bit)
        where, size = units(place, near)[unit]
        for later in range(step, chain):
            begin(a, (path + (later,), unit), span_of(where, size), orders[a][later])

    paths = [()]
    for bit in range(near, chain):
        paths = paths + [path + (bit,) for path in paths]
    for a in (0, 1):
        owned[a].wait()
        begin(a, 0, span_of(places[a], 0), orders[a][0])
    for a in (0, 1):
        spread(a, (), 0, near)
    for unit in range(near + 1):
        if unit:
            for a in (0, 1):
                arrive(a, unit - 1)
                if unit < near:
                    begin(a, unit, span_of(places[a], unit), orders[a][unit])
                spread(a, (), unit, near)
                if unit == near:
                    begin(a, "core", span_of(places[a], near), orders[a][chain])
        for path in paths[1:]:
            if path[-1] < chain - 1:
                for a in (0, 1):
                    arrive(a, (path, unit))
                    spread(a, path, unit, path[-1] + 1)
    for bit in range(near, chain - 1):
        for a in (0, 1):
            begin(a, ("core", bit), span_of(flip(places[a], bit), bit), orders[a][chain])
    for unit in range(near + 1):
        for path in paths[1:]:
            if path[-1] == chain - 1:
                for a in (0, 1):
                    arrive(a, (path, unit))
                    place = places[a]
                    for bit in path:
                        place = flip(place, bit)
                    where, size = units(place, near)[unit]
                    begin(a, ("core", path, unit), span_of(where, size), orders[a][chain])
    for a in (0, 1):
        for name, copy in copies[a].items():
            copy.wait_send()
            if (a, name) not in waited:
                copy.wait_recv()
    for fetch in fetches:
        fetch.wait()


def scatter_kernel(orders, k_in, v_in, k_out, v_out, k_acc, v_acc, k_got, v_got, k_core, v_core, send, recv):
    o, i = lax.axis_index("outer"), lax.axis_index("inner")
    rows = k_out.shape[0]
    chain = len(orders[0]) - 1
    near = sum(axis == "inner" for axis, _ in orders[0])
    greet(orders[0], o, i)
    half = 2**chain
    ins, outs, accs = (k_in, v_in), (k_out, v_out), (k_acc, v_acc)
    gots, cores = (k_got, v_got), (k_core, v_core)
    full = [place_of(order, o, i) for order in orders]
    places = [place % half for place in full]
    sides = [place // half for place in full]
    copies = ({}, {})

    def spot(place, step, offset=0):
        size = rows * 2**step
        return pl.ds(pl.multiple_of((place // 2**step) * size + offset, size), size)

    def begin(a, name, src, dst, bit):
        at = len(copies[a])
        copies[a][name] = pltpu.make_async_remote_copy(
            src_ref=src, dst_ref=dst, send_sem=send.at[a, at], recv_sem=recv.at[a, at],
            device_id=partner_of(*bit, o, i), device_id_type=MESH)
        copies[a][name].start()

    def landing(step, place, size):
        return spot(place % 2**step, size, rows * 2**step)

    def forward(a, step, name, place, size):
        begin(a, (step,) + name, accs[a].at[spot(place, size), :], gots[a].at[landing(step, place, size), :],
              orders[a][step])

    def add(a, step, place, size):
        got = gots[a][landing(step, place, size), :]
        return accs[a][spot(place, size), :].astype(jnp.float32) + got.astype(jnp.float32)

    def pieces(a):
        return [(line, near) for line in lines(flip(places[a], chain - 1), near, chain - 1)] + [
            (flip(places[a], step), step) for step in range(chain - 2, near - 1, -1)] + [(places[a], near)]

    def join(a, which):
        place, step = pieces(a)[which]
        copies[a]["core", which].wait_recv()
        mine = ins[a][spot(place, step, sides[a] * half * rows), :]
        total = mine.astype(jnp.float32) + cores[a][spot(place, step), :].astype(jnp.float32)
        accs[a][spot(place, step), :] = total.astype(jnp.bfloat16)

    ahead = 2 ** (chain - 1 - near)
    for which in range(ahead + chain - near):
        for a in (0, 1):
            place, step = pieces(a)[which]
            begin(a, ("core", which), ins[a].at[spot(place, step, (1 - sides[a]) * half * rows), :],
                  cores[a].at[spot(place, step), :], orders[a][chain])
    for at in range(ahead):
        for a in (0, 1):
            join(a, at)
            for unit in range(near, -1, -1):
                forward(a, chain - 1, (at, unit), *units(pieces(a)[at][0], near)[unit])
    for which in range(ahead, ahead + chain - near):
        for a in (0, 1):
            join(a, which)
    for step in range(chain - 1, near - 1, -1):
        count = 2 ** (step - near)
        for at in range(count):
            for unit in range(near, -1, -1):
                for a in (0, 1):
                    where, size = units(lines(places[a], near, step)[at], near)[unit]
                    copies[a][step, at, unit].wait_recv()
                    accs[a][spot(where, size), :] = add(a, step, where, size).astype(jnp.bfloat16)
                    if step > near and at < count // 2:
                        forward(a, step - 1, (at, unit), where, size)
                    elif step == near and unit == near:
                        forward(a, near - 1, (), where, size)
    for step in range(near - 1, -1, -1):
        for a in (0, 1):
            copies[a][step,].wait_recv()
            if step:
                first = flip(places[a], step - 1)
                accs[a][spot(first, step - 1), :] = add(a, step, first, step - 1).astype(jnp.bfloat16)
                forward(a, step - 1, (), first, step - 1)
                accs[a][spot(places[a], step - 1), :] = add(a, step, places[a], step - 1).astype(jnp.bfloat16)
            else:
                outs[a][...] = add(a, 0, places[a], 0).astype(jnp.bfloat16)
    for a in (0, 1):
        for copy in copies[a].values():
            copy.wait_send()


def attend_kernel(inner, blk_spans, slots_in, tab_k_in, tab_v_in, q_ref, do_ref, k_ref, v_ref,
                  dq_ref, dk_ref, dv_ref, at_k, at_v, slots, tab_k, tab_v, sem, ks, vs, *kept):
    reads = [pltpu.make_async_copy(src, dst, sem.at[j])
             for j, (src, dst) in enumerate(((slots_in, slots), (tab_k_in, tab_k), (tab_v_in, tab_v)))]
    for read in reads:
        read.start()
    spans = slots.shape[0]
    span = q_ref.shape[0] // 2
    hd = k_ref.shape[1]
    group = q_ref.shape[1] // hd
    blk = blk_spans * span
    scale = 1.0 / math.sqrt(hd)
    f32 = jnp.float32
    linear = lax.axis_index("outer") * inner + lax.axis_index("inner")

    def note(j, _):
        s = slots[j]
        at_k[s] = tab_k[j] * span
        at_v[s] = tab_v[j] * span
        return 0

    for read in reads:
        read.wait()
    lax.fori_loop(0, spans, note, 0)
    tops = [slots[2 * linear], slots[2 * linear + 1]]
    lasts = [top // blk_spans for top in tops]

    def rows_at(table, s):
        return pl.ds(pl.multiple_of(table[s], span), span)

    nt = (((1,), (1,)), ((), ()))
    tn = (((0,), (0,)), ((), ()))
    width = group * span

    def stack(ref):
        return jnp.concatenate(
            [ref[g * span:(g + 1) * span, h * hd:(h + 1) * hd] for g in (0, 1) for h in range(group)], axis=0)

    q, do = stack(q_ref), stack(do_ref)
    lane = lax.broadcasted_iota(jnp.int32, (1, 2 * width), 1)
    q_pos = lane % span + jnp.where(lane < width, tops[0], tops[1]) * span
    low = lax.broadcasted_iota(jnp.int32, (blk, 1), 0)

    def logits(k, n, first, masked):
        t = lax.dot_general(k, q[first:], nt, preferred_element_type=f32) * (scale * LOG2E)
        if masked:
            t = jnp.where(low + n * blk <= q_pos[:, first:], t, NEG_FILL)
        return t

    def stats(n, carry, first, masked, blocks=1):
        top, total, weighted = carry
        at = pl.ds(pl.multiple_of(n * blk, blk), blocks * blk)
        spots = [(n * blk_spans + j) for j in range(blocks * blk_spans)]
        k = jnp.concatenate([k_ref[rows_at(at_k, s), :] for s in spots], axis=0)
        v = jnp.concatenate([v_ref[rows_at(at_v, s), :] for s in spots], axis=0)
        ks[at, :] = k
        vs[at, :] = v
        t = logits(k, n, first, masked)
        dp = lax.dot_general(v, do[first:], nt, preferred_element_type=f32)
        new = jnp.maximum(top, jnp.max(t, axis=0, keepdims=True))
        shrink = jnp.exp2(top - new)
        e = jnp.exp2(t - new)
        if kept:
            kept[0][at, first:] = e
            kept[1][at, first:] = dp
            kept[2][n, :, first:] = new
        return (new, total * shrink + jnp.sum(e, axis=0, keepdims=True),
                weighted * shrink + jnp.sum(e * dp, axis=0, keepdims=True))

    def run(step, begin, end, first, carry):
        pairs = (end - begin) // 2
        carry = lax.fori_loop(
            0, pairs, lambda n, c: step(begin + 2 * n, c, first, False, 2), carry)
        return lax.fori_loop(begin + 2 * pairs, end, lambda n, c: step(n, c, first, False), carry)

    def sweep(step, carry, narrow):
        carry = run(step, 0, lasts[0], 0, carry)
        carry = step(lasts[0], carry, 0, True)
        late = run(step, lasts[0] + 1, lasts[1], width, narrow(carry))
        return carry, step(lasts[1], late, width, True)

    start = (jnp.full((1, 2 * width), NEG_FILL, f32), jnp.zeros((1, 2 * width), f32), jnp.zeros((1, 2 * width), f32))
    early, late = sweep(stats, start, lambda carry: tuple(x[:, width:] for x in carry))
    top, total, weighted = [jnp.concatenate([x[:, :width], y], axis=1) for x, y in zip(early, late)]
    lse = top + jnp.log2(total)
    delta = weighted / total

    def grads(n, dq, first, masked, blocks=1):
        at = pl.ds(pl.multiple_of(n * blk, blk), blocks * blk)
        k, v = ks[at, :], vs[at, :]
        if kept:
            p = kept[0][at, first:] * jnp.exp2(kept[2][n, :, first:] - lse[:, first:])
            dp = kept[1][at, first:]
        else:
            p = jnp.exp2(logits(k, n, first, masked) - lse[:, first:])
            dp = lax.dot_general(v, do[first:], nt, preferred_element_type=f32)
        ds = (p * (dp - delta[:, first:]) * scale).astype(jnp.bfloat16)
        dk = jnp.dot(ds, q[first:], preferred_element_type=f32).astype(jnp.bfloat16)
        dv = jnp.dot(p.astype(jnp.bfloat16), do[first:], preferred_element_type=f32).astype(jnp.bfloat16)
        for j in range(blocks * blk_spans):
            s = n * blk_spans + j
            dk_ref[rows_at(at_k, s), :] = dk[j * span:(j + 1) * span]
            dv_ref[rows_at(at_v, s), :] = dv[j * span:(j + 1) * span]
        return dq + lax.dot_general(k, ds, tn, preferred_element_type=f32)

    early, late = sweep(grads, jnp.zeros((hd, 2 * width), f32), lambda dq: dq[:, width:])
    dq = jnp.concatenate([early[:, :width], late], axis=1).T
    for g in (0, 1):
        for h in range(group):
            at = (g * group + h) * span
            dq_ref[g * span:(g + 1) * span, h * hd:(h + 1) * hd] = dq[at:at + span].astype(jnp.bfloat16)

    def blank(s, _):
        none = jnp.zeros((span, hd), jnp.bfloat16)
        dk_ref[rows_at(at_k, s), :] = none
        dv_ref[rows_at(at_v, s), :] = none
        return 0

    lax.fori_loop((lasts[1] + 1) * blk_spans, spans, blank, 0)


def local(outer, inner, queries, keys, values, grad_out, span_slot):
    rows, hd = keys.shape
    total = rows * outer * inner
    spans = span_slot.shape[0]
    orders = bits_of(outer, inner)
    low = jnp.bfloat16
    vmem = pl.BlockSpec(memory_space=pltpu.VMEM)
    moves = moves_of(inner.bit_length() - 1, outer.bit_length() - 2)
    hbm = pl.BlockSpec(memory_space=pltpu.HBM)
    sems = [pltpu.SemaphoreType.DMA((2, moves)), pltpu.SemaphoreType.DMA((2, moves))]
    unit = total * hd
    whole = jax.ShapeDtypeStruct((total, hd), low)
    block = jax.ShapeDtypeStruct((rows, hd), low)
    tables = [
        jnp.asarray(np.array([2 * place_of(order, j // 2 // inner, j // 2 % inner) + j % 2 for j in range(spans)], np.int32))
        for order in orders
    ]
    keys, values, queries, grad_out, *small = (
        pltpu.with_memory_space_constraint(x, pltpu.HBM)
        for x in (keys, values, queries, grad_out, span_slot, *tables))
    keys_all, values_all, queries, grad_out = pl.pallas_call(
        functools.partial(gather_kernel, orders),
        out_shape=(whole, whole) + (jax.ShapeDtypeStruct(queries.shape, low),) * 2, in_specs=[hbm] * 4, out_specs=(vmem,) * 4,
        scratch_shapes=sems + [pltpu.SemaphoreType.DMA((4,))],
        compiler_params=pltpu.CompilerParams(
            collective_id=0, has_side_effects=True, vmem_limit_bytes=4 * unit + 4 * MIB),
        cost_estimate=pl.CostEstimate(flops=0, bytes_accessed=64 * unit, transcendentals=0),
    )(keys, values, queries, grad_out)
    blk_spans = math.gcd(spans, 4)
    lanes = rows * queries.shape[1] // hd
    kept = []
    if 8 * total * lanes <= 32 * MIB:
        kept = [pltpu.VMEM((total, lanes), jnp.float32), pltpu.VMEM((total, lanes), jnp.float32),
                pltpu.VMEM((spans // blk_spans, 1, lanes), jnp.float32)]
    grad_queries, dk, dv = pl.pallas_call(
        functools.partial(attend_kernel, inner, blk_spans),
        out_shape=(jax.ShapeDtypeStruct(queries.shape, low), whole, whole),
        in_specs=[hbm] * 3 + [vmem] * 4, out_specs=(vmem, vmem, vmem),
        scratch_shapes=[pltpu.SMEM((spans,), jnp.int32)] * 5 + [pltpu.SemaphoreType.DMA((3,)),
                        pltpu.VMEM((total, hd), low), pltpu.VMEM((total, hd), low)] + kept,
        compiler_params=pltpu.CompilerParams(
            vmem_limit_bytes=12 * unit + 12 * MIB + (9 * total * lanes if kept else 0)),
    )(*small, queries, grad_out, keys_all, values_all)
    grad_keys, grad_values = pl.pallas_call(
        functools.partial(scatter_kernel, orders),
        out_shape=(block, block), in_specs=[vmem] * 2, out_specs=(vmem, vmem),
        scratch_shapes=[pltpu.VMEM((total // 2, hd), low), pltpu.VMEM((total // 2, hd), low),
                        pltpu.VMEM((total // 2, hd), low), pltpu.VMEM((total // 2, hd), low),
                        pltpu.VMEM((total // 2, hd), low), pltpu.VMEM((total // 2, hd), low)] + sems,
        compiler_params=pltpu.CompilerParams(
            collective_id=1, has_side_effects=True, vmem_limit_bytes=10 * unit + 4 * MIB),
    )(dk, dv)
    return grad_queries, grad_keys, grad_values


def solution(mesh):
    rows = P(("outer", "inner"), None)
    return jax.shard_map(
        functools.partial(local, mesh.shape["outer"], mesh.shape["inner"]),
        mesh=mesh,
        in_specs=(rows, rows, rows, rows, P()),
        out_specs=(rows, rows, rows),
        check_vma=False,
    )
```

```python
import functools
import math

import jax
import jax.numpy as jnp
import numpy as np
from jax import lax
from jax.experimental import pallas as pl
from jax.experimental.pallas import tpu as pltpu
from jax.sharding import PartitionSpec as P

NEG_FILL = -1e30
LOG2E = math.log2(math.e)
MIB = 1024 * 1024
MESH = pl.DeviceIdType.MESH


def bits_of(outer, inner):
    near = [("inner", b) for b in range(inner.bit_length() - 1)]
    chips = [("outer", b) for b in range(1, outer.bit_length() - 1)]
    core = [("outer", 0)]
    return near + chips + core, near[::-1] + chips[::-1] + core


def place_of(order, o, i):
    place = 0
    for at, (axis, b) in enumerate(order):
        place = place + (((o if axis == "outer" else i) // 2**b) % 2) * 2**at
    return place


def partner_of(axis, b, o, i):
    if axis == "outer":
        return (o + (1 - 2 * ((o // 2**b) % 2)) * 2**b, i)
    return (o, i + (1 - 2 * ((i // 2**b) % 2)) * 2**b)


def greet(order, o, i):
    barrier = pltpu.get_barrier_semaphore()
    for axis, b in order:
        pl.semaphore_signal(barrier, inc=1, device_id=partner_of(axis, b, o, i), device_id_type=MESH)
    pl.semaphore_wait(barrier, len(order))


def flip(place, step):
    return place + (1 - 2 * ((place // 2**step) % 2)) * 2**step


def units(place, near):
    return [(place, 0)] + [(flip(place, step), step) for step in range(near)]


def lines(place, near, step):
    if step == near:
        return [place]
    return lines(flip(place, step - 1), near, step - 1) + lines(place, near, step - 1)


def moves_of(near, chips):
    return near + (near + 1) * (2**chips - 1 + 2 ** (chips - 1)) + chips + 2 ** (chips - 1)


def gather_kernel(orders, k_in, v_in, q_in, do_in, k_out, v_out, q_out, do_out, send, recv, own):
    o, i = lax.axis_index("outer"), lax.axis_index("inner")
    rows = k_in.shape[0]
    chain = len(orders[0]) - 1
    near = sum(axis == "inner" for axis, _ in orders[0])
    places = [place_of(order, o, i) for order in orders]
    outs = (k_out, v_out)

    def span_of(place, step):
        size = rows * 2**step
        return pl.ds(pl.multiple_of((place // 2**step) * size, size), size)

    owned = [
        pltpu.make_async_copy((k_in, v_in)[a], outs[a].at[span_of(places[a], 0), :], own.at[a]) for a in (0, 1)
    ]
    fetches = [pltpu.make_async_copy(q_in, q_out, own.at[2]), pltpu.make_async_copy(do_in, do_out, own.at[3])]
    for copy in owned + fetches:
        copy.start()
    greet(orders[0], o, i)
    copies, waited = ({}, {}), set()

    def begin(a, name, part, bit):
        part = outs[a].at[part, :]
        at = len(copies[a])
        copies[a][name] = pltpu.make_async_remote_copy(
            src_ref=part, dst_ref=part, send_sem=send.at[a, at], recv_sem=recv.at[a, at],
            device_id=partner_of(*bit, o, i), device_id_type=MESH)
        copies[a][name].start()

    def arrive(a, name):
        copies[a][name].wait_recv()
        waited.add((a, name))

    def spread(a, path, unit, step):
        place = places[a]
        for bit in path:
            place = flip(place, bit)
        where, size = units(place, near)[unit]
        for later in range(step, chain):
            begin(a, (path + (later,), unit), span_of(where, size), orders[a][later])

    paths = [()]
    for bit in range(near, chain):
        paths = paths + [path + (bit,) for path in paths]
    for a in (0, 1):
        owned[a].wait()
        begin(a, 0, span_of(places[a], 0), orders[a][0])
    for a in (0, 1):
        spread(a, (), 0, near)
    for unit in range(near + 1):
        if unit:
            for a in (0, 1):
                arrive(a, unit - 1)
                if unit < near:
                    begin(a, unit, span_of(places[a], unit), orders[a][unit])
                spread(a, (), unit, near)
                if unit == near:
                    begin(a, "core", span_of(places[a], near), orders[a][chain])
        for path in paths[1:]:
            if path[-1] < chain - 1:
                for a in (0, 1):
                    arrive(a, (path, unit))
                    spread(a, path, unit, path[-1] + 1)
    for bit in range(near, chain - 1):
        for a in (0, 1):
            begin(a, ("core", bit), span_of(flip(places[a], bit), bit), orders[a][chain])
    for unit in range(near + 1):
        for path in paths[1:]:
            if path[-1] == chain - 1:
                for a in (0, 1):
                    arrive(a, (path, unit))
                    place = places[a]
                    for bit in path:
                        place = flip(place, bit)
                    where, size = units(place, near)[unit]
                    begin(a, ("core", path, unit), span_of(where, size), orders[a][chain])
    for a in (0, 1):
        for name, copy in copies[a].items():
            copy.wait_send()
            if (a, name) not in waited:
                copy.wait_recv()
    for fetch in fetches:
        fetch.wait()


def scatter_kernel(orders, k_in, v_in, k_out, v_out, k_acc, v_acc, k_got, v_got, k_core, v_core, send, recv):
    o, i = lax.axis_index("outer"), lax.axis_index("inner")
    rows = k_out.shape[0]
    chain = len(orders[0]) - 1
    near = sum(axis == "inner" for axis, _ in orders[0])
    greet(orders[0], o, i)
    half = 2**chain
    ins, outs, accs = (k_in, v_in), (k_out, v_out), (k_acc, v_acc)
    gots, cores = (k_got, v_got), (k_core, v_core)
    full = [place_of(order, o, i) for order in orders]
    places = [place % half for place in full]
    sides = [place // half for place in full]
    copies = ({}, {})

    def spot(place, step, offset=0):
        size = rows * 2**step
        return pl.ds(pl.multiple_of((place // 2**step) * size + offset, size), size)

    def begin(a, name, src, dst, bit):
        at = len(copies[a])
        copies[a][name] = pltpu.make_async_remote_copy(
            src_ref=src, dst_ref=dst, send_sem=send.at[a, at], recv_sem=recv.at[a, at],
            device_id=partner_of(*bit, o, i), device_id_type=MESH)
        copies[a][name].start()

    def landing(step, place, size):
        return spot(place % 2**step, size, rows * 2**step)

    def forward(a, step, name, place, size):
        begin(a, (step,) + name, accs[a].at[spot(place, size), :], gots[a].at[landing(step, place, size), :],
              orders[a][step])

    def add(a, step, place, size):
        got = gots[a][landing(step, place, size), :]
        return accs[a][spot(place, size), :].astype(jnp.float32) + got.astype(jnp.float32)

    def pieces(a):
        return [(line, near) for line in lines(flip(places[a], chain - 1), near, chain - 1)] + [
            (flip(places[a], step), step) for step in range(chain - 2, near - 1, -1)] + [(places[a], near)]

    def join(a, which):
        place, step = pieces(a)[which]
        copies[a]["core", which].wait_recv()
        mine = ins[a][spot(place, step, sides[a] * half * rows), :]
        total = mine.astype(jnp.float32) + cores[a][spot(place, step), :].astype(jnp.float32)
        accs[a][spot(place, step), :] = total.astype(jnp.bfloat16)

    ahead = 2 ** (chain - 1 - near)
    for which in range(ahead + chain - near):
        for a in (0, 1):
            place, step = pieces(a)[which]
            begin(a, ("core", which), ins[a].at[spot(place, step, (1 - sides[a]) * half * rows), :],
                  cores[a].at[spot(place, step), :], orders[a][chain])
    for at in range(ahead):
        for a in (0, 1):
            join(a, at)
            for unit in range(near, -1, -1):
                forward(a, chain - 1, (at, unit), *units(pieces(a)[at][0], near)[unit])
    for which in range(ahead, ahead + chain - near):
        for a in (0, 1):
            join(a, which)
    for step in range(chain - 1, near - 1, -1):
        count = 2 ** (step - near)
        for at in range(count):
            for unit in range(near, -1, -1):
                for a in (0, 1):
                    where, size = units(lines(places[a], near, step)[at], near)[unit]
                    copies[a][step, at, unit].wait_recv()
                    accs[a][spot(where, size), :] = add(a, step, where, size).astype(jnp.bfloat16)
                    if step > near and at < count // 2:
                        forward(a, step - 1, (at, unit), where, size)
                    elif step == near and unit == near:
                        forward(a, near - 1, (), where, size)
    for step in range(near - 1, -1, -1):
        for a in (0, 1):
            copies[a][step,].wait_recv()
            if step:
                first = flip(places[a], step - 1)
                accs[a][spot(first, step - 1), :] = add(a, step, first, step - 1).astype(jnp.bfloat16)
                forward(a, step - 1, (), first, step - 1)
                accs[a][spot(places[a], step - 1), :] = add(a, step, places[a], step - 1).astype(jnp.bfloat16)
            else:
                outs[a][...] = add(a, 0, places[a], 0).astype(jnp.bfloat16)
    for a in (0, 1):
        for copy in copies[a].values():
            copy.wait_send()


def attend_kernel(inner, blk_spans, slots_in, tab_k_in, tab_v_in, q_ref, do_ref, k_ref, v_ref,
                  dq_ref, dk_ref, dv_ref, at_k, at_v, slots, tab_k, tab_v, sem, ks, vs, *kept):
    reads = [pltpu.make_async_copy(src, dst, sem.at[j])
             for j, (src, dst) in enumerate(((slots_in, slots), (tab_k_in, tab_k), (tab_v_in, tab_v)))]
    for read in reads:
        read.start()
    spans = slots.shape[0]
    span = q_ref.shape[0] // 2
    hd = k_ref.shape[1]
    group = q_ref.shape[1] // hd
    blk = blk_spans * span
    scale = 1.0 / math.sqrt(hd)
    f32 = jnp.float32
    linear = lax.axis_index("outer") * inner + lax.axis_index("inner")

    def note(j, _):
        s = slots[j]
        at_k[s] = tab_k[j] * span
        at_v[s] = tab_v[j] * span
        return 0

    for read in reads:
        read.wait()
    lax.fori_loop(0, spans, note, 0, unroll=8)
    tops = [slots[2 * linear], slots[2 * linear + 1]]
    lasts = [top // blk_spans for top in tops]

    def rows_at(table, s):
        return pl.ds(pl.multiple_of(table[s], span), span)

    nt = (((1,), (1,)), ((), ()))
    tn = (((0,), (0,)), ((), ()))
    width = group * span

    def stack(ref):
        return jnp.concatenate(
            [ref[g * span:(g + 1) * span, h * hd:(h + 1) * hd] for g in (0, 1) for h in range(group)], axis=0)

    q, do = stack(q_ref), stack(do_ref)
    lane = lax.broadcasted_iota(jnp.int32, (1, 2 * width), 1)
    q_pos = lane % span + jnp.where(lane < width, tops[0], tops[1]) * span
    low = lax.broadcasted_iota(jnp.int32, (blk, 1), 0)

    def logits(k, n, first, masked):
        t = lax.dot_general(k, q[first:], nt, preferred_element_type=f32) * (scale * LOG2E)
        if masked:
            t = jnp.where(low + n * blk <= q_pos[:, first:], t, NEG_FILL)
        return t

    def stats(n, carry, first, masked, blocks=1):
        top, total, weighted = carry
        at = pl.ds(pl.multiple_of(n * blk, blk), blocks * blk)
        spots = [(n * blk_spans + j) for j in range(blocks * blk_spans)]
        k = jnp.concatenate([k_ref[rows_at(at_k, s), :] for s in spots], axis=0)
        v = jnp.concatenate([v_ref[rows_at(at_v, s), :] for s in spots], axis=0)
        ks[at, :] = k
        vs[at, :] = v
        t = logits(k, n, first, masked)
        dp = lax.dot_general(v, do[first:], nt, preferred_element_type=f32)
        new = jnp.maximum(top, jnp.max(t, axis=0, keepdims=True))
        shrink = jnp.exp2(top - new)
        e = jnp.exp2(t - new)
        if kept:
            kept[0][at, first:] = e
            kept[1][at, first:] = dp
            kept[2][n, :, first:] = new
        return (new, total * shrink + jnp.sum(e, axis=0, keepdims=True),
                weighted * shrink + jnp.sum(e * dp, axis=0, keepdims=True))

    def run(step, begin, end, first, carry):
        for blocks in (4, 2, 1) if first else (2, 1):
            count = (end - begin) // blocks
            carry = lax.fori_loop(
                0, count, lambda n, c, at=begin, blocks=blocks: step(at + blocks * n, c, first, False, blocks), carry)
            begin = begin + blocks * count
        return carry

    def sweep(step, carry, narrow):
        carry = run(step, 0, lasts[0], 0, carry)
        carry = step(lasts[0], carry, 0, True)
        late = run(step, lasts[0] + 1, lasts[1], width, narrow(carry))
        return carry, step(lasts[1], late, width, True)

    start = (jnp.full((1, 2 * width), NEG_FILL, f32), jnp.zeros((1, 2 * width), f32), jnp.zeros((1, 2 * width), f32))
    early, late = sweep(stats, start, lambda carry: tuple(x[:, width:] for x in carry))
    top, total, weighted = [jnp.concatenate([x[:, :width], y], axis=1) for x, y in zip(early, late)]
    lse = top + jnp.log2(total)
    delta = weighted / total

    def grads(n, dq, first, masked, blocks=1):
        at = pl.ds(pl.multiple_of(n * blk, blk), blocks * blk)
        k, v = ks[at, :], vs[at, :]
        if kept:
            p = kept[0][at, first:] * jnp.exp2(kept[2][n, :, first:] - lse[:, first:])
            dp = kept[1][at, first:]
        else:
            p = jnp.exp2(logits(k, n, first, masked) - lse[:, first:])
            dp = lax.dot_general(v, do[first:], nt, preferred_element_type=f32)
        ds = (p * (dp - delta[:, first:]) * scale).astype(jnp.bfloat16)
        dk = jnp.dot(ds, q[first:], preferred_element_type=f32).astype(jnp.bfloat16)
        dv = jnp.dot(p.astype(jnp.bfloat16), do[first:], preferred_element_type=f32).astype(jnp.bfloat16)
        for j in range(blocks * blk_spans):
            s = n * blk_spans + j
            dk_ref[rows_at(at_k, s), :] = dk[j * span:(j + 1) * span]
            dv_ref[rows_at(at_v, s), :] = dv[j * span:(j + 1) * span]
        return dq + lax.dot_general(k, ds, tn, preferred_element_type=f32)

    early, late = sweep(grads, jnp.zeros((hd, 2 * width), f32), lambda dq: dq[:, width:])
    dq = jnp.concatenate([early[:, :width], late], axis=1).T
    for g in (0, 1):
        for h in range(group):
            at = (g * group + h) * span
            dq_ref[g * span:(g + 1) * span, h * hd:(h + 1) * hd] = dq[at:at + span].astype(jnp.bfloat16)

    def blank(s, _):
        none = jnp.zeros((span, hd), jnp.bfloat16)
        dk_ref[rows_at(at_k, s), :] = none
        dv_ref[rows_at(at_v, s), :] = none
        return 0

    lax.fori_loop((lasts[1] + 1) * blk_spans, spans, blank, 0)


def local(outer, inner, queries, keys, values, grad_out, span_slot):
    rows, hd = keys.shape
    total = rows * outer * inner
    spans = span_slot.shape[0]
    orders = bits_of(outer, inner)
    low = jnp.bfloat16
    vmem = pl.BlockSpec(memory_space=pltpu.VMEM)
    moves = moves_of(inner.bit_length() - 1, outer.bit_length() - 2)
    hbm = pl.BlockSpec(memory_space=pltpu.HBM)
    sems = [pltpu.SemaphoreType.DMA((2, moves)), pltpu.SemaphoreType.DMA((2, moves))]
    unit = total * hd
    whole = jax.ShapeDtypeStruct((total, hd), low)
    block = jax.ShapeDtypeStruct((rows, hd), low)
    tables = [
        jnp.asarray(np.array([2 * place_of(order, j // 2 // inner, j // 2 % inner) + j % 2 for j in range(spans)], np.int32))
        for order in orders
    ]
    keys, values, queries, grad_out, *small = (
        pltpu.with_memory_space_constraint(x, pltpu.HBM)
        for x in (keys, values, queries, grad_out, span_slot, *tables))
    keys_all, values_all, queries, grad_out = pl.pallas_call(
        functools.partial(gather_kernel, orders),
        out_shape=(whole, whole) + (jax.ShapeDtypeStruct(queries.shape, low),) * 2, in_specs=[hbm] * 4, out_specs=(vmem,) * 4,
        scratch_shapes=sems + [pltpu.SemaphoreType.DMA((4,))],
        compiler_params=pltpu.CompilerParams(
            collective_id=0, has_side_effects=True, vmem_limit_bytes=4 * unit + 4 * MIB),
        cost_estimate=pl.CostEstimate(flops=0, bytes_accessed=64 * unit, transcendentals=0),
    )(keys, values, queries, grad_out)
    blk_spans = math.gcd(spans, 4)
    lanes = rows * queries.shape[1] // hd
    kept = []
    if 8 * total * lanes <= 32 * MIB:
        kept = [pltpu.VMEM((total, lanes), jnp.float32), pltpu.VMEM((total, lanes), jnp.float32),
                pltpu.VMEM((spans // blk_spans, 1, lanes), jnp.float32)]
    grad_queries, dk, dv = pl.pallas_call(
        functools.partial(attend_kernel, inner, blk_spans),
        out_shape=(jax.ShapeDtypeStruct(queries.shape, low), whole, whole),
        in_specs=[hbm] * 3 + [vmem] * 4, out_specs=(vmem, vmem, vmem),
        scratch_shapes=[pltpu.SMEM((spans,), jnp.int32)] * 5 + [pltpu.SemaphoreType.DMA((3,)),
                        pltpu.VMEM((total, hd), low), pltpu.VMEM((total, hd), low)] + kept,
        compiler_params=pltpu.CompilerParams(
            vmem_limit_bytes=12 * unit + 12 * MIB + (9 * total * lanes if kept else 0)),
    )(*small, queries, grad_out, keys_all, values_all)
    grad_keys, grad_values = pl.pallas_call(
        functools.partial(scatter_kernel, orders),
        out_shape=(block, block), in_specs=[vmem] * 2, out_specs=(vmem, vmem),
        scratch_shapes=[pltpu.VMEM((total // 2, hd), low), pltpu.VMEM((total // 2, hd), low),
                        pltpu.VMEM((total // 2, hd), low), pltpu.VMEM((total // 2, hd), low),
                        pltpu.VMEM((total // 2, hd), low), pltpu.VMEM((total // 2, hd), low)] + sems,
        compiler_params=pltpu.CompilerParams(
            collective_id=1, has_side_effects=True, vmem_limit_bytes=10 * unit + 4 * MIB),
    )(dk, dv)
    return grad_queries, grad_keys, grad_values


def solution(mesh):
    rows = P(("outer", "inner"), None)
    return jax.shard_map(
        functools.partial(local, mesh.shape["outer"], mesh.shape["inner"]),
        mesh=mesh,
        in_specs=(rows, rows, rows, rows, P()),
        out_specs=(rows, rows, rows),
        check_vma=False,
    )
```
